32 devices in a mesh: seq: 32 (over z, y, x, core).
Axes of the slice: x: 2, y: 2, z: 4, core: 2. Of those that a mesh axis runs over, the one named last changes fastest.
Arguments:
- hidden: bfloat16 [65536, 1024], P('seq'), may hold values from -6 to 6
- scene_lengths: int32 [16], replicated, may hold values from 1 to 32768, 65536 in all
- norm_gain: float32 [1024], replicated, may hold values from 0.1 to 1.9
- w_in: bfloat16 [1024, 4384], replicated, may hold values from -0.1875 to 0.1875
- conv_weight: float32 [4, 2304], replicated, may hold values from -3 to 3
- conv_bias: float32 [2304], replicated, may hold values from -2 to 2
- dt_bias: float32 [32], replicated, may hold values from -4.5 to -3.5
- a_log: float32 [32], replicated, may hold values from -11 to 0.7
- d_skip: float32 [32], replicated, may hold values from 0.5 to 1.5
- gate_gain: float32 [2048], replicated, may hold values from 0.1 to 1.9
- w_out: bfloat16 [2048, 1024], replicated, may hold values from -0.125 to 0.125
- out_grad: bfloat16 [65536, 1024], P('seq'), may hold values from -6 to 6
Outputs:
- mixed_out: bfloat16 [65536, 1024], P('seq')
- hidden_grad: float32 [65536, 1024], P('seq')
- norm_gain_grad: float32 [1024], replicated
- w_in_grad: float32 [1024, 4384], P('seq')
- conv_weight_grad: float32 [4, 2304], replicated
- conv_bias_grad: float32 [2304], replicated
- dt_bias_grad: float32 [32], replicated
- a_log_grad: float32 [32], replicated
- d_skip_grad: float32 [32], replicated
- gate_gain_grad: float32 [2048], replicated
- w_out_grad: float32 [2048, 1024], P(None, 'seq')
The draws below stay inside these ranges and needn't reach their ends.
Inputs may be any that keep to these rules, and one draw needn't show every extreme that they name: `scene_lengths`: scenes follow each other in the stream; they sum to 65536 tokens and the longest has exactly 32768.
All inputs are finite; a program needn't handle non-finite values.
Results may differ from the reference program's by a relative error of at most 0.0014.
The reference program's roundings to bfloat16 on the way count: a program that leaves them out, or rounds other values in their place, can miss the bound.
Values may be sent and summed in bfloat16 or wider, within the bound.
No kernel may reach another device: no remote copies, remote signals or barrier semaphores. Data moves between devices by JAX's collectives and lax.ppermute only.
A program may use at most 1.0625 GiB of HBM per device.

```python
import math
from functools import partial
import jax
import jax.numpy as jnp
import numpy as np
from jax import lax

D = 1024
H = 32
HEAD = 64
NS = 128
KW = 4
QB = 256
DI = 2048
CH = 2304
E = 4384
TOKENS = 65536
SCENES = 16
SCENE_MOST = 32768


def draw_a_log(key, part):
    wide_key = jax.random.fold_in(key, 37)
    spread = jax.random.uniform(wide_key, (H,), jnp.float32, -11.0, 0.7)
    return spread


def raised(drawn, key, source, target, blocks, factor):
    owner, partner = [(jnp.arange(drawn.shape[dim]) // (drawn.shape[dim] // blocks)).reshape([-1 if axis == dim else 1 for axis in range(drawn.ndim)]) for dim in (source, target)]
    chosen = jax.random.permutation(key, blocks)[partner]
    strong = (owner == chosen) | (owner == (partner + blocks // 2) % blocks)
    return jnp.where(strong, factor * drawn, drawn)


def block_scale(rng, dims, cuts, least, top_value):
    def one(dim, shards_of):
        draws = jax.random.uniform(jax.random.fold_in(jax.random.fold_in(rng, 6), dim), (shards_of,), jnp.float32, least / len(cuts), top_value / len(cuts))
        return jnp.repeat(jnp.exp(draws), dims[dim] // shards_of).reshape((-1,) + (1,) * (len(dims) - dim - 1))

    level = one(*cuts[0])
    for cut in cuts[1:]:
        level = level * one(*cut)
    return level


def profile(number_of, total, bound, lean):
    loads = [(1 << 20) // math.isqrt(rank ** lean) + 1 for rank in range(2, number_of + 1)]
    rest, holding = total - bound - (number_of - 1), [1] * (number_of - 1)
    while rest > 0:
        free = [i for i in range(number_of - 1) if holding[i] < bound]
        whole, left = sum([loads[i] for i in free]), rest
        for i in free:
            more = min(bound - holding[i], max(1, left * loads[i] // whole), rest)
            holding[i] = holding[i] + more
            rest = rest - more
    return np.array([bound] + holding)


def ragged(own_key, count, total, reach, lean):
    if count == 2:
        one = jax.random.randint(own_key, (), max(1, total - reach), min(reach, total - 1) + 1)
        return jnp.stack([one, total - one])
    sizes = jnp.asarray(profile(count, total, reach, lean), jnp.int32)
    couples = (count - 1) // 2
    donor, receiver = sizes[1:1 + 2 * couples:2], sizes[2:2 + 2 * couples:2]
    margin = jnp.minimum(donor - 1, reach - receiver)
    shifted = jax.random.randint(jax.random.fold_in(own_key, 1), (couples,), 0, 1 << 20) % (margin + 1)
    sizes = sizes.at[1:1 + 2 * couples:2].set(donor - shifted).at[2:2 + 2 * couples:2].set(receiver + shifted)
    return sizes[jax.random.permutation(jax.random.fold_in(own_key, 2), count)]


def gaussian(key, dims, deviation, reach, shards=(), kind=jnp.bfloat16):
    drawn = jax.random.normal(key, dims, jnp.float32) * deviation
    if len(shards) > 0:
        drawn = block_scale(key, dims, shards, -0.22, 0.18) * drawn
    return jnp.clip(drawn, min=-reach, max=reach).astype(kind)


def heavy_noise(rng, extent, deviation, most, cuts, heavy, held_as=jnp.bfloat16):
    entries = deviation * jax.random.normal(rng, extent, jnp.float32)
    if cuts:
        entries = entries * block_scale(rng, extent, cuts, -0.22, 0.18)
    return jnp.clip(raised(entries, jax.random.fold_in(rng, 3), *heavy), -most, most).astype(held_as)


def setup_inputs(seed: int = 0) -> dict:
    seeds = jax.random.split(jax.random.key(seed), 13)
    return {
        "hidden": heavy_noise(seeds[0], (TOKENS, D), 1.0, 6.0, ((0, 32),), (0, 1, 32, 2.75)),
        "scene_lengths": ragged(seeds[1], SCENES, TOKENS, SCENE_MOST, 2).astype(jnp.int32),
        "norm_gain": jnp.clip(1.0 + 0.18 * jax.random.normal(seeds[2], (D,), jnp.float32), 0.1, 1.9),
        "w_in": gaussian(seeds[3], (D, E), D ** -0.5, 0.1875),
        "conv_weight": gaussian(seeds[4], (KW, CH), KW ** -0.5, 3.0, (), jnp.float32),
        "conv_bias": gaussian(seeds[5], (CH,), 0.5, 2.0, (), jnp.float32),
        "dt_bias": jnp.clip(jax.random.uniform(seeds[6], (H,), jnp.float32, -4.5, -3.5), -4.5, -3.5),
        "a_log": draw_a_log(jax.random.fold_in(seeds[12], 71), 0),
        "d_skip": jnp.clip(jax.random.uniform(seeds[8], (H,), jnp.float32, 0.5, 1.5), 0.5, 1.5),
        "gate_gain": jnp.clip(1.0 + 0.18 * jax.random.normal(seeds[9], (DI,), jnp.float32), 0.1, 1.9),
        "w_out": gaussian(seeds[10], (DI, D), DI ** -0.5, 0.125),
        "out_grad": heavy_noise(seeds[11], (TOKENS, D), 1.0, 6.0, ((0, 32),), (0, 1, 32, 2.75)),
    }


norm_eps = 1e-05
highest = lax.Precision.HIGHEST

@jax.custom_vjp
def low(v):
    return lax.optimization_barrier(v.astype(jnp.bfloat16)).astype(jnp.float32)

@jax.custom_vjp
def low_back(v):
    return v

def low_keep(v):
    return (low(v), None)

def low_pass(kept, grad):
    return (grad,)

def back_keep(v):
    return (v, None)

def back_low(kept, grad):
    return (low(grad),)
low.defvjp(low_keep, low_pass)
low_back.defvjp(back_keep, back_low)

def scene_marks(starts, position):
    before = starts[None, :] <= position[:, None]
    begins = lax.optimization_barrier(jnp.max(jnp.where(before, starts[None, :], 0), axis=1)).astype(jnp.int32)
    resets = jnp.any(starts[None, :] == position[:, None], axis=1)
    return (begins, resets)

def rms_scale(values, gain_row):
    return values * lax.rsqrt(lax.optimization_barrier(jnp.mean(values * values, axis=1, keepdims=True)) + norm_eps) * gain_row

def mix_block(params, starts, running, inputs):
    w_in, w_out, norm_gain, conv_weight, conv_bias, dt_bias, a_log, d_skip, gate_gain = params
    state_in, rim_rows = running
    hidden_block, position = inputs
    normed = rms_scale(hidden_block, norm_gain)
    projected = low_back(jnp.dot(low(normed), w_in, precision=highest))
    gate_z = projected[:, :DI]
    xbc_low = low(projected[:, DI:DI + CH])
    dt_raw = projected[:, DI + CH:]
    extended = jnp.concatenate([rim_rows, xbc_low], axis=0)
    begins, resets = scene_marks(starts, position)
    conv_sum = jnp.zeros((QB, CH), jnp.float32) + conv_bias
    for tap_index in range(KW):
        valid_taps = (position - (KW - 1 - tap_index) >= begins).astype(jnp.float32)
        conv_sum = conv_sum + conv_weight[tap_index] * extended[tap_index:tap_index + QB] * valid_taps[:, None]
    activated = jax.nn.silu(conv_sum)
    x_heads = activated[:, :DI].reshape(QB, H, HEAD)
    b_rows = activated[:, DI:DI + NS]
    c_rows = activated[:, DI + NS:]
    step_size = jax.nn.softplus(dt_raw + dt_bias)
    log_decay = jnp.cumsum(step_size * -jnp.exp(a_log), axis=0)
    segment = jnp.cumsum(resets.astype(jnp.int32))
    ordering = jnp.arange(QB)
    same_scene = (segment[:, None] == segment[None, :]) & (ordering[:, None] >= ordering[None, :])
    decay_gaps = log_decay[:, None, :] - log_decay[None, :, :]
    weights = jnp.exp(jnp.where(same_scene[:, :, None], decay_gaps, -jnp.inf))
    scores = jnp.dot(c_rows, b_rows.T, precision=highest)
    mixing = scores[:, :, None] * weights * step_size[None, :, :]
    inside = jnp.einsum('tsh,shp->thp', mixing, x_heads, precision=highest)
    carry_live = (segment == 0).astype(jnp.float32)
    carried = jnp.einsum('tn,hpn->thp', c_rows, state_in, precision=highest) * (jnp.exp(log_decay) * carry_live[:, None])[:, :, None]
    ssd_out = inside + carried + d_skip[None, :, None] * x_heads
    tail_live = (segment == segment[-1]).astype(jnp.float32)
    tail_weight = jnp.exp(log_decay[-1][None, :] - log_decay) * tail_live[:, None] * step_size
    opened = (segment[-1] == 0).astype(jnp.float32)
    new_state = state_in * (jnp.exp(log_decay[-1]) * opened)[:, None, None] + jnp.einsum('shp,sn->hpn', tail_weight[:, :, None] * x_heads, b_rows, precision=highest)
    gated = ssd_out.reshape(QB, DI) * jax.nn.silu(gate_z)
    mixed = jnp.dot(low(rms_scale(gated, gate_gain)), w_out, precision=highest)
    return ((new_state, xbc_low[QB - (KW - 1):]), hidden_block + mixed)

def reference(hidden, scene_lengths, norm_gain, w_in, conv_weight, conv_bias, dt_bias, a_log, d_skip, gate_gain, w_out, out_grad):
    starts = (jnp.cumsum(scene_lengths) - scene_lengths).astype(jnp.int32)
    positions = jnp.arange(TOKENS, dtype=jnp.int32).reshape(TOKENS // QB, QB)
    params = (w_in.astype(jnp.float32), w_out.astype(jnp.float32), norm_gain, conv_weight, conv_bias, dt_bias, a_log, d_skip, gate_gain)

    def forward(hidden_full, weights_all):
        block_step = jax.checkpoint(partial(mix_block, weights_all, starts))
        initial = (jnp.zeros((H, HEAD, NS), jnp.float32), jnp.zeros((KW - 1, CH), jnp.float32))
        _, blocks = lax.scan(block_step, initial, (hidden_full.reshape(TOKENS // QB, QB, D), positions))
        return blocks.reshape(TOKENS, D)
    result, pullback = jax.vjp(forward, hidden.astype(jnp.float32), params)
    hidden_grad, weight_grads = pullback(out_grad.astype(jnp.float32))
    w_in_grad, w_out_grad, norm_gain_grad, conv_weight_grad, conv_bias_grad, dt_bias_grad, a_log_grad, d_skip_grad, gate_gain_grad = weight_grads
    return (result.astype(jnp.bfloat16), hidden_grad, norm_gain_grad, w_in_grad, conv_weight_grad, conv_bias_grad, dt_bias_grad, a_log_grad, d_skip_grad, gate_gain_grad, w_out_grad)
```

```python
import functools

import jax
import jax.numpy as jnp
from jax import lax
from jax.experimental import pallas as pl
from jax.experimental.pallas import tpu as pltpu
from jax.sharding import PartitionSpec as P

Q = 128
LANES = 128
EPS = 1e-05
LOG2E = 1.4426950408889634
f32 = jnp.float32
bf16 = jnp.bfloat16
VMEM_BYTES = 60 << 20


def mm(a, b):
    return lax.dot_general(a, b, (((1,), (0,)), ((), ())), preferred_element_type=f32)


def mm_nt(a, b):
    return lax.dot_general(a, b, (((1,), (1,)), ((), ())), preferred_element_type=f32)


def mm_tn(a, b):
    return lax.dot_general(a, b, (((0,), (0,)), ((), ())), preferred_element_type=f32)


def split2(v):
    hi = v.astype(bf16)
    return hi, (v - hi.astype(f32)).astype(bf16)


def sigmoid(v):
    return 1.0 / (1.0 + jnp.exp(-v))


def lane_iota(rows):
    return lax.broadcasted_iota(jnp.int32, (rows, LANES), 1)


def spread(v, heads):
    hi = v.astype(bf16).astype(f32)
    rest = v - hi
    mid = rest.astype(bf16).astype(f32)
    low = rest - mid
    lane = lane_iota(v.shape[0])
    kept = jnp.where(lane < heads, hi, jnp.where(lane < 2 * heads, mid, low))
    return jnp.where(lane < 3 * heads, kept, 0.0).astype(bf16)


def exact3(v):
    hi = v.astype(bf16)
    rest = v - hi.astype(f32)
    mid = rest.astype(bf16)
    return hi, mid, (rest - mid.astype(f32)).astype(bf16)


def mask_mm(mask, v):
    hi, mid, low = exact3(v)
    return mm(mask, hi) + mm(mask, mid) + mm(mask, low)


def prod3(a_hi, a_lo, b_hi, b_lo):
    left = jnp.concatenate([a_hi, a_lo], axis=1)
    return mm(left, jnp.concatenate([b_hi, b_hi], axis=0)) + mm(a_hi, b_lo)


def head_sums(v, red):
    hi, lo = split2(v)
    return mm(hi, red) + mm(lo, red)


def tri_masks(begin_col, begin_row):
    row = lax.broadcasted_iota(jnp.int32, (Q, Q), 0)
    col = lax.broadcasted_iota(jnp.int32, (Q, Q), 1)
    same = jnp.broadcast_to(begin_col, (Q, Q)) == jnp.broadcast_to(begin_row, (Q, Q))
    return same & (row >= col), same & (row <= col)


def project_kernel(
    heads, inner, state,
    hid, rim, gain, w_x, w_bc, w_dt, cw, cb, dtb, alog, meta, expm,
    nl_o, xbc_o, x_o, bc_o, dsil_o, step_o, sig_o, la_o, cum_o, sloc_o, dst_o, ddec_o,
    ext, srun, cum,
):
    rows = hid.shape[0]
    channels = inner + 2 * state
    step_id = pl.program_id(0)

    @pl.when(step_id == 0)
    def _():
        ext[0:8, :] = rim[...]
        srun[...] = jnp.zeros_like(srun)
        cum[...] = jnp.zeros_like(cum)

    hv = hid[...].astype(f32)
    mean = jnp.mean(hv * hv, axis=1, keepdims=True)
    nl = (hv * lax.rsqrt(mean + EPS) * gain[...]).astype(bf16)
    nl_o[...] = nl

    v = mm(nl, w_dt[...]) + dtb[...]
    step = jnp.maximum(v, 0.0) + jnp.log1p(jnp.exp(-jnp.abs(v)))
    step_o[...] = step
    sig_o[...] = sigmoid(v)
    rate = -step * (jnp.exp(alog[...]) * LOG2E)

    m1, m2, m3 = meta[:, 1:2], meta[:, 2:3], meta[:, 3:4]
    width = 256
    for g in range(channels // width):
        cols = slice(g * width, (g + 1) * width)
        weights = w_x[:, cols] if g * width < inner else w_bc[...]
        low = mm(nl, weights).astype(bf16)
        xbc_o[:, cols] = low
        ext[8 : 8 + rows, cols] = low.astype(f32)
        conv = cb[:, cols] + cw[3:4, cols] * ext[8 : 8 + rows, cols]
        conv = conv + cw[2:3, cols] * (ext[7 : 7 + rows, cols] * m1)
        conv = conv + cw[1:2, cols] * (ext[6 : 6 + rows, cols] * m2)
        conv = conv + cw[0:1, cols] * (ext[5 : 5 + rows, cols] * m3)
        gate = sigmoid(conv)
        act = conv * gate
        dsil_o[:, cols] = gate + act * (1.0 - gate)
        if g * width < inner:
            x_o[:, cols] = act
        else:
            bc_o[...] = act
    ext[0:8, :] = ext[rows : rows + 8, :]

    row = lax.broadcasted_iota(jnp.int32, (Q, Q), 0)
    col = lax.broadcasted_iota(jnp.int32, (Q, Q), 1)
    tri = (row >= col).astype(bf16)
    for c in range(rows // Q):
        rs = slice(c * Q, (c + 1) * Q)
        la = mask_mm(tri, rate[rs])
        la_o[rs, :] = la
        cum_o[c * 8 : (c + 1) * 8, :] = cum[...]
        last = la[Q - 1 : Q, :]
        cum[...] = cum[...] + last
        weight = jnp.exp2(last - la) * meta[rs, 7:8] * step[rs]
        decay = jnp.exp2(last) * meta[c * Q + Q - 1 : c * Q + Q, 8:9]
        decay_x = mm(spread(jnp.broadcast_to(decay, (8, LANES)), heads), expm[...])
        weight_s = spread(weight, heads)
        bt_hi, bt_lo = split2(bc_o[rs, :state].T)
        for g in range(inner // width):
            cols = slice(g * width, (g + 1) * width)
            wx = x_o[rs, cols] * mm(weight_s, expm[:, cols])
            hi, lo = split2(wx)
            new = prod3(bt_hi, bt_lo, hi, lo)
            old = srun[:, cols]
            sloc_o[c, :, cols] = old
            srun[:, cols] = old * decay_x[0:1, cols] + new
        if c == rows // Q - 1:
            @pl.when(step_id == pl.num_programs(0) - 1)
            def _():
                live = meta[c * Q + Q - 1 : c * Q + Q, 9:10]
                total = jnp.exp2(cum[...]) * live
                ddec_o[...] = mm(spread(total, heads), expm[...])
                dst_o[...] = srun[...]


def scan_kernel(
    heads, inner, state,
    x, bc, step, la_r, meta, brow, sloc, nl, w_z, expm,
    y_o, z_o,
    usc,
):
    la = la_r[...]
    la_t = la.T
    mask, _ = tri_masks(meta[:, 0:1], brow[0])
    b_hi, b_lo = split2(bc[:, :state])
    c_hi, c_lo = split2(bc[:, state:])
    c_cat = jnp.concatenate([c_hi, c_lo], axis=1)
    scores = mm_nt(c_cat, jnp.concatenate([b_hi, b_hi], axis=1)) + mm_nt(c_hi, b_lo)
    scores = jnp.where(mask, scores, 0.0)
    step_s = spread(step[...], heads)
    carry_s = spread(jnp.exp2(la) * meta[:, 8:9], heads)
    lane = lane_iota(Q)
    head_width = inner // heads
    for j in range(inner // LANES):
        cols = slice(j * LANES, (j + 1) * LANES)
        u_hi, u_lo = split2(x[:, cols] * mm(step_s, expm[:, cols]))
        u_cat = jnp.concatenate([u_hi, u_lo], axis=1)
        right = jnp.concatenate([u_cat, u_cat], axis=0)
        lefts = []
        for e in range(2):
            h = 2 * j + e
            gap = jnp.minimum(la[:, h : h + 1] - la_t[h : h + 1, :], 0.0)
            w_hi, w_lo = split2(scores * jnp.exp2(gap))
            lefts.append(jnp.concatenate([w_hi, w_lo], axis=1))
        both = mm(jnp.concatenate(lefts, axis=0), right)
        both = both[:, :LANES] + both[:, LANES:]
        y = jnp.where(lane < head_width, both[:Q], both[Q:])
        s_hi, s_lo = split2(sloc[0, :, cols])
        carried = mm(c_cat, jnp.concatenate([s_hi, s_hi], axis=0)) + mm(c_hi, s_lo)
        y_o[:, cols] = y + carried * mm(carry_s, expm[:, cols])
    nlv = nl[...]
    for g in range(inner // 256):
        cols = slice(g * 256, (g + 1) * 256)
        z_o[:, cols] = mm(nlv, w_z[:, cols])


def gate_kernel(
    heads, inner, state,
    yss, x, z, og, w_out, s_in, bc, la_r, cum, meta, dsk, gain, expm, red,
    gl_o, dy_o, gz_o, rowdot_o, sin_o, dgain_o, dskip_o,
    gsc, ysc, ggsc, ssc,
):
    step_id = pl.program_id(0)

    @pl.when(step_id == 0)
    def _():
        sin_o[...] = jnp.zeros_like(sin_o)
        dgain_o[...] = jnp.zeros_like(dgain_o)
        dskip_o[...] = jnp.zeros_like(dskip_o)
        hi, lo = split2(s_in[...])
        ssc[0:state, :] = hi
        ssc[state : 2 * state, :] = hi
        ssc[2 * state :, :] = lo

    c_hi, c_lo = split2(bc[:, state:])
    c_cat = jnp.concatenate([c_hi, c_lo], axis=1)
    ct_hi, ct_lo = split2(bc[:, state:].T)
    enter_s = spread(jnp.exp2(la_r[...] + cum[0:1, :]) * meta[:, 9:10], heads)
    ogv = og[...]
    width = 256
    sq = jnp.zeros((Q, LANES), f32)
    dotted = jnp.zeros((Q, LANES), f32)
    for g in range(inner // width):
        cols = slice(g * width, (g + 1) * width)
        gg = mm_nt(ogv, w_out[cols, :])
        carried = mm(c_cat, ssc[0 : 2 * state, cols]) + mm(c_hi, ssc[2 * state :, cols])
        y = yss[:, cols] + carried * mm(enter_s, expm[:, cols])
        ysc[:, cols] = y
        zv = z[:, cols]
        gated = (y + dsk[:, cols] * x[:, cols]) * (zv * sigmoid(zv))
        gsc[:, cols] = gated
        ggsc[:, cols] = gg
        s = gated * gated
        d = gg * gain[:, cols] * gated
        for k in range(width // LANES):
            sq = sq + s[:, k * LANES : (k + 1) * LANES]
            dotted = dotted + d[:, k * LANES : (k + 1) * LANES]
    mean = jnp.sum(sq, axis=1, keepdims=True) / inner
    r = lax.rsqrt(mean + EPS)
    m = jnp.sum(dotted, axis=1, keepdims=True) / inner
    coeff = r * r * r * m
    rowdot = jnp.zeros((Q, LANES), f32)
    for g in range(inner // width):
        cols = slice(g * width, (g + 1) * width)
        gated = gsc[:, cols]
        gg = ggsc[:, cols]
        gn = gated * r
        gl_o[:, cols] = (gn * gain[:, cols]).astype(bf16)
        dgain_o[0:1, cols] += jnp.sum(gg * gn, axis=0, keepdims=True)
        grad_gated = r * (gain[:, cols] * gg) - gated * coeff
        zv = z[:, cols]
        sg = sigmoid(zv)
        sz = zv * sg
        dy = grad_gated * sz
        dy_o[:, cols] = dy
        ys = ysc[:, cols]
        xv = x[:, cols]
        gz_o[:, cols] = (
            grad_gated * (ys + dsk[:, cols] * xv) * (sg + sz * (1.0 - sg))
        ).astype(bf16)
        rowdot = rowdot + head_sums(dy * ys, red[cols, :])
        dskip_o[0:1, cols] += jnp.sum(dy * xv, axis=0, keepdims=True)
        hi, lo = split2(dy * mm(enter_s, expm[:, cols]))
        sin_o[:, cols] += prod3(ct_hi, ct_lo, hi, lo)
    rowdot_o[...] = rowdot


def back_kernel(
    heads, inner, state,
    x, bc, step_r, sig, la_r, cum, meta, brow, sloc, s_in, dyr, rowdot, dsil, xbc,
    d_in, s_out, dsk, cw, alog, expm, red,
    pg_o, dt_o, first_o, tail_o, dcw_o, small_o,
    ds, cgx, xb, wgt,
):
    step_id = pl.program_id(0)
    channels = inner + 2 * state

    @pl.when(step_id == 0)
    def _():
        ds[...] = d_in[...]
        cgx[Q:, :] = jnp.zeros_like(cgx[Q:, :])
        dcw_o[...] = jnp.zeros_like(dcw_o)
        small_o[...] = jnp.zeros_like(small_o)
        total = jnp.sum(d_in[...] * s_out[...], axis=0, keepdims=True)
        xb[...] = head_sums(jnp.broadcast_to(total, (8, inner)), red[...])

    @pl.when(step_id > 0)
    def _():
        cgx[Q:, :] = cgx[0:8, :]

    la = la_r[...]
    la_t = la.T
    mask, mask_t = tri_masks(meta[:, 0:1], brow[0])
    b32, c32 = bc[:, :state], bc[:, state:]
    b_hi, b_lo = split2(b32)
    c_hi, c_lo = split2(c32)
    b_cat = jnp.concatenate([b_hi, b_lo], axis=1)
    ct_hi, ct_lo = split2(c32.T)
    scores_t = mm_nt(b_cat, jnp.concatenate([c_hi, c_hi], axis=1)) + mm_nt(b_hi, c_lo)
    scores_t = jnp.where(mask_t, scores_t, 0.0)
    step = step_r[...]
    last = la[Q - 1 : Q, :]
    tail = meta[:, 7:8]
    step_s = spread(step, heads)
    carry_s = spread(jnp.exp2(la) * meta[:, 8:9], heads)
    tail_s = spread(jnp.exp2(last - la) * tail, heads)
    decay = jnp.exp2(last) * meta[Q - 1 : Q, 8:9]
    enter = jnp.exp2(cum[0:1, :]) * meta[0:1, 9:10]
    decay_s = spread(jnp.broadcast_to(decay, (8, LANES)), heads)
    enter_s = spread(jnp.broadcast_to(enter, (8, LANES)), heads)
    lane = lane_iota(Q)
    left_half = lane < inner // heads
    zero = jnp.zeros((Q, LANES), bf16)

    dg_t = jnp.zeros((Q, Q), f32)
    dc = jnp.zeros((Q, 2 * state), f32)
    db = jnp.zeros((Q, 2 * state), f32)
    xdu = jnp.zeros((Q, LANES), f32)
    xacc = jnp.zeros((8, LANES), f32)
    for j in range(inner // LANES):
        cols = slice(j * LANES, (j + 1) * LANES)
        xv = x[:, cols]
        dy = dyr[:, cols]
        step_x = mm(step_s, expm[:, cols])
        carry_x = mm(carry_s, expm[:, cols])
        tail_x = mm(tail_s, expm[:, cols])
        u = xv * step_x
        u_hi, u_lo = split2(u)
        dy_hi, dy_lo = split2(dy)
        dy_cat = jnp.concatenate([dy_hi, dy_lo], axis=1)
        rows = []
        for e in range(2):
            keep = left_half if e == 0 else ~left_half
            rows.append(
                jnp.concatenate([jnp.where(keep, u_hi, zero), jnp.where(keep, u_lo, zero)], axis=1)
            )
        right = jnp.concatenate(
            [jnp.concatenate([dy_hi, dy_hi], axis=1), jnp.concatenate([dy_lo, dy_lo], axis=1)], axis=0
        )
        dw = mm_nt(jnp.concatenate(rows, axis=0), right)
        dw = dw[:, :Q] + dw[:, Q:]
        lefts = []
        for e in range(2):
            h = 2 * j + e
            gap = jnp.minimum(la_t[h : h + 1, :] - la[:, h : h + 1], 0.0)
            decays = jnp.exp2(gap)
            w_hi, w_lo = split2(scores_t * decays)
            lefts.append(jnp.concatenate([w_hi, w_lo], axis=1))
            dg_t = dg_t + dw[e * Q : (e + 1) * Q] * decays
        both = mm(jnp.concatenate(lefts, axis=0), jnp.concatenate([dy_cat, dy_cat], axis=0))
        both = both[:, :LANES] + both[:, LANES:]
        du = jnp.where(left_half, both[:Q], both[Q:])
        d_out = ds[:, cols]
        d_hi, d_lo = split2(d_out)
        du = du + tail_x * (mm(b_cat, jnp.concatenate([d_hi, d_hi], axis=0)) + mm(b_hi, d_lo))
        xdu = xdu + head_sums(xv * du, red[cols, :])
        dx = dsk[:, cols] * dy + step_x * du
        cgx[0:Q, cols] = dx * dsil[:, cols]
        enter_x = mm(enter_s, expm[:, cols])[0:1]
        s_true = sloc[0, :, cols] + enter_x * s_in[:, cols]
        s_hi, s_lo = split2(s_true)
        v_hi, v_lo = split2(carry_x * dy)
        t_hi, t_lo = split2(tail_x * u)
        s_cat = jnp.concatenate([s_hi, s_lo], axis=0)
        d_cat = jnp.concatenate([d_hi, d_lo], axis=0)
        dc = dc + mm_nt(v_hi, s_cat) + mm_nt(v_lo, s_cat)
        db = db + mm_nt(t_hi, d_cat) + mm_nt(t_lo, d_cat)
        decay_x = mm(decay_s, expm[:, cols])[0:1]
        d_new = d_out * decay_x + prod3(ct_hi, ct_lo, v_hi, v_lo)
        ds[:, cols] = d_new
        total = jnp.sum(d_new * s_true, axis=0, keepdims=True)
        xacc = xacc + head_sums(jnp.broadcast_to(total, (8, LANES)), red[cols, :])

    g_hi, g_lo = split2(jnp.where(mask_t, dg_t, 0.0))
    db_all = db[:, :state] + db[:, state:] + (
        mm(g_hi, c_hi) + mm(g_lo, c_hi) + mm(g_hi, c_lo)
    )
    dc_all = dc[:, :state] + dc[:, state:] + (
        mm_tn(g_hi, b_hi) + mm_tn(g_lo, b_hi) + mm_tn(g_hi, b_lo)
    )
    cgx[0:Q, inner : inner + state] = db_all * dsil[:, inner : inner + state]
    cgx[0:Q, inner + state :] = dc_all * dsil[:, inner + state :]

    flow = rowdot[...] - step * xdu
    g = mask_mm(mask_t.astype(bf16), flow) + tail * xb[0:1, :]
    g = g * meta[:, 10:11]
    rate = jnp.exp(alog[...])
    dt = (xdu - g * rate) * sig[...]
    dt_o[...] = dt.astype(bf16)
    small_o[0:1, :] += jnp.sum(-g * step * rate, axis=0, keepdims=True)
    small_o[1:2, :] += jnp.sum(dt, axis=0, keepdims=True)
    xb[...] = xacc

    m1, m2, m3 = meta[:, 4:5], meta[:, 5:6], meta[:, 6:7]
    width = 128
    for k in range(channels // width):
        cols = slice(k * width, (k + 1) * width)
        e0 = cgx[0:Q, cols]
        e1 = cgx[1 : Q + 1, cols] * m1
        e2 = cgx[2 : Q + 2, cols] * m2
        e3 = cgx[3 : Q + 3, cols] * m3
        grad = cw[3:4, cols] * e0 + cw[2:3, cols] * e1 + cw[1:2, cols] * e2 + cw[0:1, cols] * e3
        pg_o[:, cols] = grad.astype(bf16)
        xf = xbc[:, cols].astype(f32)
        for tap, e in ((3, e0), (2, e1), (1, e2), (0, e3)):
            dcw_o[tap : tap + 1, cols] += jnp.sum(xf * e, axis=0, keepdims=True)
        dcw_o[4:5, cols] += jnp.sum(e0, axis=0, keepdims=True)

        @pl.when(step_id == 0)
        def _():
            tail_o[:, cols] = grad[Q - 8 :, :]

    @pl.when(step_id == pl.num_programs(0) - 1)
    def _():
        first_o[...] = cgx[0:8, :]


def chain_kernel(backward, pieces, out):
    count = pieces.shape[0]
    rows = out.shape[1]

    def turn(i, run):
        k = count - 1 - i if backward else i
        out[k] = run
        return run * pieces[k, rows : rows + 1, :] + pieces[k, 0:rows, :]

    lax.fori_loop(0, count, turn, jnp.zeros(out.shape[1:], f32))


def params(**more):
    return pltpu.CompilerParams(vmem_limit_bytes=VMEM_BYTES, **more)


def exchange(local, decay, backward):
    count = lax.axis_size("seq")
    rows, lanes = local.shape
    split = max(1, count // rows)
    per, width = rows * split // count, lanes // split
    parts = local.reshape(count, per, width)
    decays = jnp.tile(decay.reshape(split, 1, width), (count // split, 1, 1))
    parts = jnp.concatenate([parts, decays], axis=1)
    got = lax.all_to_all(parts, "seq", 0, 0, tiled=True)
    out = pl.pallas_call(
        functools.partial(chain_kernel, backward),
        out_shape=jax.ShapeDtypeStruct((count, per, width), f32),
        compiler_params=params(),
    )(got)
    return lax.all_to_all(out, "seq", 0, 0, tiled=True).reshape(rows, lanes)


def from_behind(value, steps):
    count = lax.axis_size("seq")
    first, last = max(0, -steps), min(count, count - steps)
    return lax.ppermute(value, "seq", [(s, s + steps) for s in range(first, last)])


def body(
    hidden, scene_lengths, norm_gain, w_in, conv_weight, conv_bias, dt_bias, a_log, d_skip,
    gate_gain, w_out, out_grad,
):
    tokens, model = hidden.shape
    heads = a_log.shape[0]
    inner = gate_gain.shape[0]
    channels = conv_bias.shape[0]
    state = (channels - inner) // 2
    chunks = tokens // Q
    repeat = LANES // heads
    columns = w_in.shape[1]

    scenes = scene_lengths.shape[0]
    order = jnp.arange(scenes)
    starts = jnp.sum(jnp.where(order[None, :] < order[:, None], scene_lengths[None, :], 0), axis=1)
    dev_start = lax.axis_index("seq") * tokens
    wide_pos = dev_start + jnp.arange(tokens + 8, dtype=jnp.int32)
    begin_all = jnp.max(jnp.where(starts[None, :] <= wide_pos[:, None], starts[None, :], 0), axis=1)
    begin, pos = begin_all[:tokens], wide_pos[:tokens]
    chunk_last = jnp.repeat(begin.reshape(chunks, Q)[:, -1], Q)
    chunk_start = pos // Q * Q
    inside = jnp.arange(tokens)
    notes = [
        begin,
        pos - 1 >= begin,
        pos - 2 >= begin,
        pos - 3 >= begin,
        (begin_all[1 : tokens + 1] <= pos) & (inside + 1 < tokens),
        (begin_all[2 : tokens + 2] <= pos) & (inside + 2 < tokens),
        (begin_all[3 : tokens + 3] <= pos) & (inside + 3 < tokens),
        begin == chunk_last,
        begin < chunk_start,
        begin < dev_start,
        begin != pos,
    ]
    meta = jnp.stack([n.astype(f32) for n in notes] + [jnp.zeros((tokens,), f32)] * (16 - len(notes)), axis=1)
    brow = begin.astype(f32).reshape(chunks, 1, Q)

    head_of = jnp.arange(inner) // (inner // heads)
    expm = (jnp.arange(LANES)[:, None] % heads == head_of[None, :]).astype(bf16)
    red = expm.T

    def four(v):
        return jnp.tile(v, repeat).reshape(1, LANES)

    gain_row = norm_gain.reshape(1, model)
    w_dt = jnp.tile(w_in[:, inner + channels :], (1, repeat))
    dsk = jnp.repeat(d_skip, inner // heads).reshape(1, inner)
    cb = conv_bias.reshape(1, channels)
    gate_row = gate_gain.reshape(1, inner)

    edge = hidden[tokens - 8 :].astype(f32)
    edge_low = (
        edge * lax.rsqrt(jnp.mean(edge * edge, axis=1, keepdims=True) + EPS) * norm_gain
    ).astype(bf16)
    edge_xbc = jnp.dot(
        edge_low, w_in[:, inner : inner + channels], preferred_element_type=f32
    ).astype(bf16)
    rim = from_behind(edge_xbc, 1).astype(f32)

    tb = 2 * Q
    whole = lambda shape: pl.BlockSpec(shape, lambda i: (0,) * len(shape), pipeline_mode=pl.Buffered(1))
    rowsb = lambda n, width: pl.BlockSpec((n, width), lambda i: (i, 0))
    sds = jax.ShapeDtypeStruct
    (nl, xbc, x, bc, dsil, step, sig, la, cum, sloc, dev_state, dev_decay) = pl.pallas_call(
        functools.partial(project_kernel, heads, inner, state),
        grid=(tokens // tb,),
        in_specs=[
            rowsb(tb, model), whole((8, channels)), whole((1, model)),
            pl.BlockSpec((model, inner), lambda i: (0, 1), pipeline_mode=pl.Buffered(1)),
            pl.BlockSpec((model, 2 * state), lambda i: (0, 2 * inner // (2 * state)), pipeline_mode=pl.Buffered(1)),
            whole((model, LANES)), whole((4, channels)), whole((1, channels)), whole((1, LANES)),
            whole((1, LANES)), rowsb(tb, 16), whole((LANES, inner)),
        ],
        out_specs=[
            rowsb(tb, model), rowsb(tb, channels), rowsb(tb, inner), rowsb(tb, 2 * state),
            rowsb(tb, channels), rowsb(tb, LANES), rowsb(tb, LANES), rowsb(tb, LANES),
            rowsb(tb // Q * 8, LANES), pl.BlockSpec((tb // Q, state, inner), lambda i: (i, 0, 0)),
            pl.BlockSpec((state, inner), lambda i: (0, 0)), pl.BlockSpec((8, inner), lambda i: (0, 0)),
        ],
        out_shape=[
            sds((tokens, model), bf16), sds((tokens, channels), bf16), sds((tokens, inner), f32),
            sds((tokens, 2 * state), f32), sds((tokens, channels), f32), sds((tokens, LANES), f32),
            sds((tokens, LANES), f32), sds((tokens, LANES), f32), sds((chunks * 8, LANES), f32),
            sds((chunks, state, inner), f32), sds((state, inner), f32), sds((8, inner), f32),
        ],
        scratch_shapes=[
            pltpu.VMEM((tb + 8, channels), f32), pltpu.VMEM((state, inner), f32), pltpu.VMEM((8, LANES), f32),
        ],
        compiler_params=params(),
    )(hidden, rim, gain_row, w_in, w_in, w_dt, conv_weight, cb, four(dt_bias), four(a_log), meta, expm)

    state_in = exchange(dev_state, dev_decay[0:1], False)

    yss, z = pl.pallas_call(
        functools.partial(scan_kernel, heads, inner, state),
        grid=(chunks,),
        in_specs=[
            rowsb(Q, inner), rowsb(Q, 2 * state), rowsb(Q, LANES), rowsb(Q, LANES), rowsb(Q, 16),
            pl.BlockSpec((1, 1, Q), lambda i: (i, 0, 0)),
            pl.BlockSpec((1, state, inner), lambda i: (i, 0, 0)),
            rowsb(Q, model), whole((model, inner)), whole((LANES, inner)),
        ],
        out_specs=[rowsb(Q, inner), rowsb(Q, inner)],
        out_shape=[sds((tokens, inner), f32), sds((tokens, inner), f32)],
        scratch_shapes=[pltpu.VMEM((8, LANES), f32)],
        compiler_params=params(),
    )(x, bc, step, la, meta, brow, sloc, nl, w_in, expm)

    gate_low, dy, gz, rowdot, state_in_grad, dgain, dskip = pl.pallas_call(
        functools.partial(gate_kernel, heads, inner, state),
        grid=(chunks,),
        in_specs=[
            rowsb(Q, inner), rowsb(Q, inner), rowsb(Q, inner), rowsb(Q, model), whole((inner, model)),
            whole((state, inner)), rowsb(Q, 2 * state), rowsb(Q, LANES), rowsb(8, LANES), rowsb(Q, 16),
            whole((1, inner)), whole((1, inner)), whole((LANES, inner)), whole((inner, LANES)),
        ],
        out_specs=[
            rowsb(Q, inner), rowsb(Q, inner), rowsb(Q, inner), rowsb(Q, LANES),
            pl.BlockSpec((state, inner), lambda i: (0, 0)), pl.BlockSpec((8, inner), lambda i: (0, 0)),
            pl.BlockSpec((8, inner), lambda i: (0, 0)),
        ],
        out_shape=[
            sds((tokens, inner), bf16), sds((tokens, inner), f32), sds((tokens, inner), bf16),
            sds((tokens, LANES), f32), sds((state, inner), f32), sds((8, inner), f32), sds((8, inner), f32),
        ],
        scratch_shapes=[
            pltpu.VMEM((Q, inner), f32), pltpu.VMEM((Q, inner), f32), pltpu.VMEM((Q, inner), f32),
            pltpu.VMEM((3 * state, inner), bf16),
        ],
        compiler_params=params(),
    )(yss, x, z, out_grad, w_out, state_in, bc, la, cum, meta, dsk, gate_row, expm, red)

    state_out_grad = exchange(state_in_grad, dev_decay[0:1], True)
    state_out = dev_state + dev_decay[0:1] * state_in

    mixed_out = (hidden.astype(f32) + jnp.dot(gate_low, w_out, preferred_element_type=f32)).astype(bf16)
    w_out_part = jnp.einsum("tk,ti->ki", out_grad, gate_low, preferred_element_type=f32)
    w_out_grad = lax.psum_scatter(w_out_part, "seq", scatter_dimension=0, tiled=True).T

    final = chunks - 1
    back = lambda n, width: pl.BlockSpec((n, width), lambda i: (final - i, 0))
    pg, dt_grad, first, tail, dcw, small = pl.pallas_call(
        functools.partial(back_kernel, heads, inner, state),
        grid=(chunks,),
        in_specs=[
            back(Q, inner), back(Q, 2 * state), back(Q, LANES), back(Q, LANES), back(Q, LANES),
            back(8, LANES), back(Q, 16), pl.BlockSpec((1, 1, Q), lambda i: (final - i, 0, 0)),
            pl.BlockSpec((1, state, inner), lambda i: (final - i, 0, 0)), whole((state, inner)),
            back(Q, inner), back(Q, LANES), back(Q, channels), back(Q, channels),
            whole((state, inner)), whole((state, inner)), whole((1, inner)), whole((4, channels)),
            whole((1, LANES)), whole((LANES, inner)), whole((inner, LANES)),
        ],
        out_specs=[
            back(Q, channels), back(Q, LANES),
            pl.BlockSpec((8, channels), lambda i: (0, 0)), pl.BlockSpec((8, channels), lambda i: (0, 0)),
            pl.BlockSpec((8, channels), lambda i: (0, 0)), pl.BlockSpec((8, LANES), lambda i: (0, 0)),
        ],
        out_shape=[
            sds((tokens, channels), bf16), sds((tokens, LANES), bf16), sds((8, channels), f32),
            sds((8, channels), f32), sds((8, channels), f32), sds((8, LANES), f32),
        ],
        scratch_shapes=[
            pltpu.VMEM((state, inner), f32), pltpu.VMEM((Q + 8, channels), f32), pltpu.VMEM((8, LANES), f32),
            pltpu.VMEM((8, LANES), f32),
        ],
        compiler_params=params(),
    )(
        x, bc, step, sig, la, cum, meta, brow, sloc, state_in, dy, rowdot, dsil, xbc,
        state_out_grad, state_out, dsk, conv_weight, four(a_log), expm, red,
    )

    rim_grad = from_behind(first, -1)
    last_pos = wide_pos[tokens - 3 : tokens]
    last_low = xbc[tokens - 3 :].astype(f32)
    cross = jnp.zeros((3, channels), f32)
    cross_taps = [jnp.zeros((channels,), f32)]
    for j in (3, 2, 1):
        count = j
        rows_here = jnp.arange(3 - count, 3)
        ok = (begin_all[tokens - 3 + 3 - count + j : tokens + j] <= last_pos[3 - count :]).astype(f32)
        e = rim_grad[0:count] * ok[:, None]
        cross = cross.at[3 - count :].add(conv_weight[3 - j] * e)
        cross_taps.append(jnp.sum(last_low[3 - count :] * e, axis=0))
    conv_weight_part = dcw[0:4] + jnp.stack(cross_taps[1:] + cross_taps[:1], axis=0)
    is_last = lax.axis_index("seq") == lax.axis_size("seq") - 1
    fixed = (tail + jnp.pad(cross, ((5, 0), (0, 0)))).astype(bf16)
    pg = lax.dynamic_update_slice(pg, jnp.where(is_last, tail.astype(bf16), fixed), (tokens - 8, 0))

    projected_grad = jnp.concatenate([gz, pg, dt_grad[:, :heads]], axis=1)
    normed_grad = jnp.einsum("te,de->td", projected_grad, w_in, preferred_element_type=f32)
    w_in_part = jnp.einsum("tk,te->ke", nl, projected_grad, preferred_element_type=f32)
    w_in_grad = lax.psum_scatter(w_in_part, "seq", scatter_dimension=0, tiled=True)

    hv = hidden.astype(f32)
    s = lax.rsqrt(jnp.mean(hv * hv, axis=1, keepdims=True) + EPS)
    gained = normed_grad * norm_gain
    inner_mean = jnp.mean(gained * hv, axis=1, keepdims=True)
    hidden_grad = out_grad.astype(f32) + s * gained - hv * (s * s * s * inner_mean)
    norm_gain_part = jnp.sum(normed_grad * hv * s, axis=0)

    dskip_part = jnp.sum(dskip[0].reshape(heads, inner // heads), axis=1)
    summed = lax.psum(
        (norm_gain_part, conv_weight_part, dcw[4], small[1, :heads], small[0, :heads], dskip_part, dgain[0]),
        "seq",
    )
    return (
        mixed_out, hidden_grad, summed[0], w_in_grad, summed[1], summed[2], summed[3], summed[4],
        summed[5], summed[6], w_out_grad,
    )


def solution(mesh):
    rep = P()
    return jax.shard_map(
        body,
        mesh=mesh,
        in_specs=(P("seq", None),) + (rep,) * 10 + (P("seq", None),),
        out_specs=(P("seq", None), P("seq", None), rep, P("seq", None), rep, rep, rep, rep, rep, rep, P(None, "seq")),
        check_vma=False,
    )
```

```python
import functools

import jax
import jax.numpy as jnp
import numpy as np
from jax import lax
from jax.experimental import pallas as pl
from jax.experimental.pallas import tpu as pltpu
from jax.sharding import PartitionSpec as P

Q = 128
LANES = 128
EPS = 1e-05
LOG2E = 1.4426950408889634
f32 = jnp.float32
bf16 = jnp.bfloat16
VMEM_BYTES = 60 << 20
SUB = 2
WIDE = 256


def mm(a, b):
    return lax.dot_general(a, b, (((1,), (0,)), ((), ())), preferred_element_type=f32)


def mm_nt(a, b):
    return lax.dot_general(a, b, (((1,), (1,)), ((), ())), preferred_element_type=f32)


def mm_tn(a, b):
    return lax.dot_general(a, b, (((0,), (0,)), ((), ())), preferred_element_type=f32)


def split2(v):
    hi = v.astype(bf16)
    return hi, (v - hi.astype(f32)).astype(bf16)


def sigmoid(v):
    return jax.nn.sigmoid(v)


def lane_iota(rows):
    return lax.broadcasted_iota(jnp.int32, (rows, LANES), 1)


def spread(v, heads):
    hi = v.astype(bf16).astype(f32)
    rest = v - hi
    mid = rest.astype(bf16).astype(f32)
    low = rest - mid
    lane = lane_iota(v.shape[0])
    kept = jnp.where(lane < heads, hi, jnp.where(lane < 2 * heads, mid, low))
    return jnp.where(lane < 3 * heads, kept, 0.0).astype(bf16)


def exact3(v):
    hi = v.astype(bf16)
    rest = v - hi.astype(f32)
    mid = rest.astype(bf16)
    return hi, mid, (rest - mid.astype(f32)).astype(bf16)


def mask_mm(mask, v):
    hi, mid, low = exact3(v)
    return mm(mask, hi) + mm(mask, mid) + mm(mask, low)


def prod3(a_hi, a_lo, b_hi, b_lo):
    left = jnp.concatenate([a_hi, a_lo], axis=1)
    return mm(left, jnp.concatenate([b_hi, b_hi], axis=0)) + mm(a_hi, b_lo)


def head_sums(v, red):
    hi, lo = split2(v)
    return mm(hi, red) + mm(lo, red)


def tri_masks(begin_col, begin_row):
    row = lax.broadcasted_iota(jnp.int32, (Q, Q), 0)
    col = lax.broadcasted_iota(jnp.int32, (Q, Q), 1)
    same = jnp.broadcast_to(begin_col, (Q, Q)) == jnp.broadcast_to(begin_row, (Q, Q))
    return same & (row >= col), same & (row <= col)


def project_kernel(
    heads, inner, state,
    hid, rim, gain, w_x, w_bc, w_dt, cw, cb, dtb, alog, meta, expm,
    nl_o, xbc_o, x_o, bc_o, dsil_o, step_o, sig_o, la_o, cum_o, decay_o, sloc_o, dst_o,
    ext, srun, cum, msk,
):
    rows = hid.shape[0]
    channels = inner + 2 * state
    step_id = pl.program_id(0)

    @pl.when(step_id == 0)
    def _():
        ext[0:8, :] = rim[...]
        srun[...] = jnp.zeros_like(srun)
        cum[...] = jnp.zeros_like(cum)

    hv = hid[...].astype(f32)
    mean = jnp.mean(hv * hv, axis=1, keepdims=True)
    nl = (hv * lax.rsqrt(mean + EPS) * gain[...]).astype(bf16)
    nl_o[...] = nl

    v = mm(nl, w_dt[...]) + dtb[...]
    step = jnp.maximum(v, 0.0) + jnp.log1p(jnp.exp(-jnp.abs(v)))
    step_o[...] = step
    sig_o[...] = 1.0 / (1.0 + jnp.exp(-v))
    rate = -step * (jnp.exp(alog[...]) * LOG2E)

    for j in range(3):
        msk[j] = jnp.broadcast_to(meta[:, 1 + j : 2 + j], (rows, LANES))
    m1, m2, m3 = (jnp.concatenate([msk[j]] * (WIDE // LANES), axis=1) for j in range(3))
    for g in range(channels // WIDE):
        cols = slice(g * WIDE, (g + 1) * WIDE)
        weights = w_x[cols, :] if g * WIDE < inner else w_bc[...]
        low = mm_nt(nl, weights).astype(bf16)
        xbc_o[:, cols] = low
        ext[8 : 8 + rows, cols] = low.astype(f32)
        conv = cb[:, cols] + cw[3:4, cols] * ext[8 : 8 + rows, cols]
        conv = conv + cw[2:3, cols] * (ext[7 : 7 + rows, cols] * m1)
        conv = conv + cw[1:2, cols] * (ext[6 : 6 + rows, cols] * m2)
        conv = conv + cw[0:1, cols] * (ext[5 : 5 + rows, cols] * m3)
        gate = sigmoid(conv)
        act = conv * gate
        dsil_o[:, cols] = gate + act * (1.0 - gate)
        if g * WIDE < inner:
            x_o[:, cols] = act
        else:
            bc_o[...] = act
    ext[0:8, :] = ext[rows : rows + 8, :]

    row = lax.broadcasted_iota(jnp.int32, (Q, Q), 0)
    col = lax.broadcasted_iota(jnp.int32, (Q, Q), 1)
    tri = (row >= col).astype(bf16)
    for c in range(rows // Q):
        rs = slice(c * Q, (c + 1) * Q)
        la = mask_mm(tri, rate[rs])
        la_o[rs, :] = la
        enter = jnp.exp2(cum[...]) * meta[c * Q : c * Q + 1, 9:10]
        cum_o[c * 8 : (c + 1) * 8, :] = cum[...]
        last = la[Q - 1 : Q, :]
        cum[...] = cum[...] + last
        weight = jnp.exp2(last - la) * meta[rs, 7:8] * step[rs]
        decay = jnp.exp2(last) * meta[c * Q + Q - 1 : c * Q + Q, 8:9]
        sub = lax.broadcasted_iota(jnp.int32, (8, LANES), 0)
        both = jnp.where(sub == 0, jnp.broadcast_to(decay, (8, LANES)), enter)
        factors = jnp.concatenate([spread(weight, heads), spread(both, heads), jnp.zeros((8, LANES), bf16)], axis=0)
        b_t = bc_o[rs, :state].T
        bt_hi, bt_lo = split2(b_t)
        for g in range(inner // WIDE):
            cols = slice(g * WIDE, (g + 1) * WIDE)
            wide = mm(factors, expm[:, cols])
            decay_o[c * 8 : (c + 1) * 8, cols] = wide[Q : Q + 8]
            hi, lo = split2(x_o[rs, cols] * wide[:Q])
            new = prod3(bt_hi, bt_lo, hi, lo)
            old = srun[:, cols]
            sloc_o[c, :, cols] = old
            srun[:, cols] = old * wide[Q : Q + 1] + new
        if c == rows // Q - 1:
            @pl.when(step_id == pl.num_programs(0) - 1)
            def _():
                live = meta[c * Q + Q - 1 : c * Q + Q, 9:10]
                total = jnp.exp2(cum[...]) * live
                dst_o[:, :inner] = srun[...]
                dst_o[:, inner:] = jnp.broadcast_to(total[0:1], (state, LANES))


def over_heads(v, first, count, half):
    shape = (v.shape[0], LANES)
    column = lambda h: jnp.broadcast_to(v[:, h : h + 1], shape)
    pairs = [jnp.where(half, column(h), column(h + 1)) for h in range(first, first + count, 2)]
    return jnp.concatenate(pairs, axis=1)


def scan_kernel(heads, inner, state, x_r, bc_r, step_r, la_rows, meta_r, brow, sloc, expm, y_o):
    left_half = lane_iota(Q) < inner // heads
    for c in range(SUB):
        rs = slice(c * Q, (c + 1) * Q)
        la = la_rows[rs, :]
        la_t = la.T
        meta, step = meta_r[rs, :], step_r[rs, :]
        mask, _ = tri_masks(meta[:, 0:1], brow[c])
        b_hi, b_lo = split2(bc_r[rs, :state])
        c_hi, c_lo = split2(bc_r[rs, state:])
        c_cat = jnp.concatenate([c_hi, c_lo], axis=1)
        scores = mm_nt(c_cat, jnp.concatenate([b_hi, b_hi], axis=1)) + mm_nt(c_hi, b_lo)
        scores = jnp.where(mask, scores, 0.0)
        carry_s = spread(jnp.exp2(la) * meta[:, 8:9], heads)
        for k in range(inner // WIDE):
            wide_cols = slice(k * WIDE, (k + 1) * WIDE)
            first = k * WIDE * heads // inner
            s_hi, s_lo = split2(sloc[c, :, wide_cols])
            carried = mm(carry_s, expm[:, wide_cols]) * (
                mm(c_cat, jnp.concatenate([s_hi, s_hi], axis=0)) + mm(c_hi, s_lo)
            )
            step_x = over_heads(step, first, WIDE * heads // inner, left_half)
            all_hi, all_lo = split2(x_r[rs, wide_cols] * step_x)
            for p in range(WIDE // LANES):
                own = slice(p * LANES, (p + 1) * LANES)
                cols = slice(k * WIDE + p * LANES, k * WIDE + (p + 1) * LANES)
                u_cat = jnp.concatenate([all_hi[:, own], all_lo[:, own]], axis=1)
                right = jnp.concatenate([u_cat, u_cat], axis=0)
                lefts = []
                for e in range(2):
                    h = first + 2 * p + e
                    gap = jnp.minimum(la[:, h : h + 1] - la_t[h : h + 1, :], 0.0)
                    w_hi, w_lo = split2(scores * jnp.exp2(gap))
                    lefts.append(jnp.concatenate([w_hi, w_lo], axis=1))
                both = mm(jnp.concatenate(lefts, axis=0), right)
                both = both[:, :LANES] + both[:, LANES:]
                y_o[rs, cols] = jnp.where(left_half, both[:Q], both[Q:]) + carried[:, own]


def gate_kernel(
    heads, inner, state,
    yss, x, z, og, w_out, s_in, bc, la_r, cum, meta, dsk, gain, expm, red,
    gl_o, dy_o, gz_o, rowdot_o, sin_o, dgain_o, dskip_o,
    gsc, ysc, ssc, exs, grad, ogs,
):
    step_id = pl.program_id(0)
    rows = x.shape[0]

    @pl.when(step_id == 0)
    def _():
        sin_o[:, :inner] = jnp.zeros((state, inner), f32)
        dgain_o[...] = jnp.zeros_like(dgain_o)
        dskip_o[...] = jnp.zeros_like(dskip_o)
        ogs[...] = jnp.zeros_like(ogs)
        hi, lo = split2(s_in[...])
        ssc[0:state, :] = hi
        ssc[state : 2 * state, :] = hi
        ssc[2 * state :, :] = lo

    c_hi, c_lo = split2(bc[:, state:])
    c_cat = jnp.concatenate([c_hi, c_lo], axis=1)
    ct_hi, ct_lo = split2(bc[:, state:].T)
    before = jnp.concatenate(
        [jnp.broadcast_to(cum[8 * c : 8 * c + 1, :], (Q, LANES)) for c in range(rows // Q)], axis=0
    )
    enter_s = spread(jnp.exp2(la_r[...] + before) * meta[:, 9:10], heads)
    ogv = og[...]
    ogs[...] += eights(jnp.square(ogv.astype(f32)))
    sq = jnp.zeros((rows, LANES), f32)
    dotted = jnp.zeros((rows, LANES), f32)
    for g in range(inner // WIDE):
        cols = slice(g * WIDE, (g + 1) * WIDE)
        carried = mm(c_cat, ssc[0 : 2 * state, cols]) + mm(c_hi, ssc[2 * state :, cols])
        enter_x = mm(enter_s, expm[:, cols])
        exs[:, cols] = enter_x
        y = yss[:, cols] + carried * enter_x
        ysc[:, cols] = y
        zv = z[:, cols]
        gated = (y + dsk[:, cols] * x[:, cols]) * (zv * sigmoid(zv))
        gsc[:, cols] = gated
        s = gated * gated
        gg = mm_nt(ogv, w_out[cols, :])
        grad[:, cols] = gg
        d = gg * gain[:, cols] * gated
        for k in range(WIDE // LANES):
            sq = sq + s[:, k * LANES : (k + 1) * LANES]
            dotted = dotted + d[:, k * LANES : (k + 1) * LANES]
    mean = jnp.sum(sq, axis=1, keepdims=True) / inner
    r = lax.rsqrt(mean + EPS)
    m = jnp.sum(dotted, axis=1, keepdims=True) / inner
    coeff = r * r * r * m
    rowdot = jnp.zeros((2 * rows, LANES), f32)
    for g in range(inner // WIDE):
        cols = slice(g * WIDE, (g + 1) * WIDE)
        gated = gsc[:, cols]
        gg = grad[:, cols]
        gn = gated * r
        gl_o[:, cols] = (gn * gain[:, cols]).astype(bf16)
        dgain_o[0:1, cols] += jnp.sum(gg * gn, axis=0, keepdims=True)
        grad_gated = r * (gain[:, cols] * gg) - gated * coeff
        zv = z[:, cols]
        sg = sigmoid(zv)
        sz = zv * sg
        dy = grad_gated * sz
        dy_o[:, cols] = dy
        ys = ysc[:, cols]
        xv = x[:, cols]
        gz = grad_gated * (ys + dsk[:, cols] * xv) * (sg + sz * (1.0 - sg))
        gz_o[:, cols] = gz.astype(bf16)
        dgain_o[1:2, cols] += jnp.sum(gz * gz, axis=0, keepdims=True)
        rowdot = rowdot + mm(jnp.concatenate(split2(dy * ys), axis=0), red[cols, :])
        dskip_o[0:1, cols] += jnp.sum(dy * xv, axis=0, keepdims=True)
        hi, lo = split2(dy * exs[:, cols])
        sin_o[:, cols] += mm(ct_hi, hi) + mm(ct_lo, hi) + mm(ct_hi, lo)
    rowdot_o[...] = rowdot[:rows] + rowdot[rows:]

    @pl.when(step_id == pl.num_programs(0) - 1)
    def _():
        most = jnp.max(dgain_o[1:2, :], axis=1, keepdims=True)
        og_most = jnp.max(jnp.sum(ogs[...], axis=0, keepdims=True), axis=1, keepdims=True)
        sin_o[:, inner:] = jnp.where(lane_iota(state) < LANES // 2, most, og_most)


def back_kernel(
    heads, head_width, state, first_head, started, into, last_one,
    x, bc, step_r, la_r, decay, meta, brow, sloc, s_in, dyr, dsil, xbc,
    d_in, s_out, dsk, cw, expm, red, *rest,
):
    if started:
        acc_in, rest = rest[:2], rest[2:]
    if last_one:
        (sig, rowdot, alog), rest = rest[:3], rest[3:]
    if into:
        rest = rest[1:]
    if last_one:
        pg_o, par_o, first_o, tail_o, dcw_o, ds, cgx, tot, msk = rest
    else:
        pg_o, dcb_o, small_o, first_o, tail_o, dcw_o, ds, cgx, tot, msk = rest
    step_id = pl.program_id(0)
    width = x.shape[1]
    rows = SUB * Q

    @pl.when(step_id == 0)
    def _():
        ds[...] = d_in[...]
        cgx[0:8, :] = jnp.zeros_like(cgx[0:8, :])
        dcw_o[...] = jnp.zeros_like(dcw_o)
        if last_one:
            par_o[...] = jnp.zeros_like(par_o)
        for p in range(width // LANES):
            cols = slice(p * LANES, (p + 1) * LANES)
            tot[p : p + 1, :] = jnp.sum(d_in[:, cols] * s_out[:, cols], axis=0, keepdims=True)

    cgx[rows:, :] = cgx[0:8, :]
    pairs = width // LANES
    left_half = lane_iota(Q) < head_width
    zero = jnp.zeros((Q, LANES), bf16)
    lane8 = lane_iota(8)
    pair8 = lax.broadcasted_iota(jnp.int32, (8, LANES), 0)
    for c in reversed(range(SUB)):
        rs = slice(c * Q, (c + 1) * Q)
        part = tot[0:8, :]
        halves = [
            jnp.sum(jnp.where(side, part, 0.0), axis=1, keepdims=True)
            for side in (lane8 < head_width, lane8 >= head_width)
        ]
        ends = jnp.zeros((8, LANES), f32)
        for e in range(2):
            here = (lane8 % heads == first_head + 2 * pair8 + e) & (pair8 < pairs)
            ends = ends + jnp.where(here, halves[e], 0.0)
        ends = jnp.sum(ends, axis=0, keepdims=True)

        la = la_r[rs, :]
        la_t = la.T
        notes = meta[rs, :]
        for j in range(3):
            msk[j] = jnp.broadcast_to(notes[:, 4 + j : 5 + j], (Q, LANES))
        _, mask_t = tri_masks(notes[:, 0:1], brow[c])
        b_hi, b_lo = split2(bc[rs, :state])
        c32 = bc[rs, state:]
        c_hi, c_lo = split2(c32)
        b_cat = jnp.concatenate([b_hi, b_lo], axis=1)
        ct_hi, ct_lo = split2(c32.T)
        scores_t = mm_nt(b_cat, jnp.concatenate([c_hi, c_hi], axis=1)) + mm_nt(b_hi, c_lo)
        scores_t = jnp.where(mask_t, scores_t, 0.0)
        last = la[Q - 1 : Q, :]
        tail = notes[:, 7:8]
        step = step_r[rs, :]
        tail_v = jnp.exp2(last - la) * tail
        factors = jnp.concatenate(
            [spread(step, heads), spread(jnp.exp2(la) * notes[:, 8:9], heads)], axis=0
        )

        dg_t = jnp.zeros((Q, Q), f32)
        dc = jnp.zeros((Q, state), f32)
        db = jnp.zeros((Q, state), f32)
        xdu = jnp.zeros((Q, LANES), f32)
        for lo_col in range(0, width, WIDE):
            wd = min(WIDE, width - lo_col)
            wcols = slice(lo_col, lo_col + wd)
            first = first_head + lo_col // head_width
            wide = mm(factors, expm[:, wcols])
            step_x, carry_x = wide[:Q], wide[Q:]
            tail_x = over_heads(tail_v, first, wd // head_width, left_half)
            xv = x[rs, wcols]
            dy = dyr[rs, wcols]
            u = xv * step_x
            u_hi, u_lo = split2(u)
            dy_hi, dy_lo = split2(dy)
            d_out = ds[:, wcols]
            d_hi, d_lo = split2(d_out)
            through = tail_x * (mm(b_cat, jnp.concatenate([d_hi, d_hi], axis=0)) + mm(b_hi, d_lo))
            insides = []
            for p in range(wd // LANES):
                own = slice(p * LANES, (p + 1) * LANES)
                uh, ul, yh, yl = u_hi[:, own], u_lo[:, own], dy_hi[:, own], dy_lo[:, own]
                sides = []
                for e in range(2):
                    keep = left_half if e == 0 else ~left_half
                    sides.append(
                        jnp.concatenate([jnp.where(keep, uh, zero), jnp.where(keep, ul, zero)], axis=1)
                    )
                right = jnp.concatenate(
                    [jnp.concatenate([yh, yh], axis=1), jnp.concatenate([yl, yl], axis=1)], axis=0
                )
                dw = mm_nt(jnp.concatenate(sides, axis=0), right)
                dw = dw[:, :Q] + dw[:, Q:]
                lefts = []
                for e in range(2):
                    h = first + 2 * p + e
                    gap = jnp.minimum(la_t[h : h + 1, :] - la[:, h : h + 1], 0.0)
                    decays = jnp.exp2(gap)
                    w_hi, w_lo = split2(scores_t * decays)
                    lefts.append(jnp.concatenate([w_hi, w_lo], axis=1))
                    dg_t = dg_t + dw[e * Q : (e + 1) * Q] * decays
                y_cat = jnp.concatenate([yh, yl], axis=1)
                both = mm(jnp.concatenate(lefts, axis=0), jnp.concatenate([y_cat, y_cat], axis=0))
                both = both[:, :LANES] + both[:, LANES:]
                insides.append(jnp.where(left_half, both[:Q], both[Q:]))
            du = through + (jnp.concatenate(insides, axis=1) if len(insides) > 1 else insides[0])
            sums = mm(jnp.concatenate(split2(xv * du), axis=0), red[wcols, :])
            xdu = xdu + sums[:Q] + sums[Q:]
            cgx[rs, wcols] = (dsk[:, wcols] * dy + step_x * du) * dsil[rs, wcols]
            s_true = sloc[c, :, wcols] + decay[8 * c + 1 : 8 * c + 2, wcols] * s_in[:, wcols]
            s_hi, s_lo = split2(s_true)
            v_hi, v_lo = split2(carry_x * dy)
            t_hi, t_lo = split2(tail_x * u)
            res = mm_nt(jnp.concatenate([v_hi, v_lo], axis=0), jnp.concatenate([s_hi, s_lo], axis=0))
            dc = dc + (res[:Q, :state] + res[:Q, state:] + res[Q:, :state])
            res = mm_nt(jnp.concatenate([t_hi, t_lo], axis=0), jnp.concatenate([d_hi, d_lo], axis=0))
            db = db + (res[:Q, :state] + res[:Q, state:] + res[Q:, :state])
            d_new = d_out * decay[8 * c : 8 * c + 1, wcols] + prod3(ct_hi, ct_lo, v_hi, v_lo)
            ds[:, wcols] = d_new
            total = jnp.sum(d_new * s_true, axis=0, keepdims=True)
            for p in range(wd // LANES):
                row = lo_col // LANES + p
                tot[row : row + 1, :] = total[:, p * LANES : (p + 1) * LANES]
            conv_back(c, wcols, msk, cgx, cw, xbc, pg_o, dcw_o, tail_o)

        parts = [dg_t, dc, db, xdu]
        if started:
            parts = [v + acc_in[0][rs, i * LANES : (i + 1) * LANES] for i, v in enumerate(parts)]
            ends = ends + acc_in[1][8 * c : 8 * c + 1, :]
        if not last_one:
            for i, value in enumerate(parts):
                dcb_o[rs, i * LANES : (i + 1) * LANES] = value
            small_o[8 * c : 8 * c + 8, :] = jnp.broadcast_to(ends, (8, LANES))
            continue
        dg_t, dc, db, xdu = parts
        g_hi, g_lo = split2(jnp.where(mask_t, dg_t, 0.0))
        dc = dc + mm_tn(g_hi, b_hi) + mm_tn(g_lo, b_hi) + mm_tn(g_hi, b_lo)
        db = db + mm(g_hi, c_hi) + mm(g_lo, c_hi) + mm(g_hi, c_lo)
        cgx[rs, width : width + state] = db * dsil[rs, width : width + state]
        cgx[rs, width + state :] = dc * dsil[rs, width + state :]
        flow = rowdot[rs, :] - step * xdu
        g = mask_mm(mask_t.astype(bf16), flow) + tail * ends
        g = g * notes[:, 10:11]
        rate = jnp.exp(alog[...])
        dt = (xdu - g * rate) * sig[rs, :]
        used = cgx.shape[1]
        pg_o[rs, used : used + LANES] = jnp.where(lane_iota(Q) < heads, dt, 0.0).astype(bf16)
        pg_o[rs, used + LANES :] = jnp.zeros((Q, pg_o.shape[1] - used - LANES), bf16)
        par_o[0:1, :] += jnp.sum(-g * step * rate, axis=0, keepdims=True)
        par_o[1:2, :] += jnp.sum(dt, axis=0, keepdims=True)
        par_o[2:3, :] += jnp.sum(dt * dt, axis=0, keepdims=True)
        conv_back(c, slice(width, width + 2 * state), msk, cgx, cw, xbc, pg_o, dcw_o, tail_o)
    first_o[...] = cgx[0:8, :]


def eights(v):
    return jnp.sum(v.reshape(v.shape[0] // 8, 8, v.shape[1]), axis=0)


def conv_back(c, which, msk, cgx, cw, xbc, pg_o, dcw_o, tail_o):
    at = c * Q
    for start in range(which.start, which.stop, LANES):
        cols = slice(start, start + LANES)
        e0 = cgx[at : at + Q, cols]
        e1 = cgx[at + 1 : at + Q + 1, cols] * msk[0]
        e2 = cgx[at + 2 : at + Q + 2, cols] * msk[1]
        e3 = cgx[at + 3 : at + Q + 3, cols] * msk[2]
        grad = cw[3:4, cols] * e0 + cw[2:3, cols] * e1 + cw[1:2, cols] * e2 + cw[0:1, cols] * e3
        pg_o[at : at + Q, cols] = grad.astype(bf16)
        xf = xbc[at : at + Q, cols].astype(f32)
        for tap, e in ((3, e0), (2, e1), (1, e2), (0, e3)):
            dcw_o[8 * tap : 8 * tap + 8, cols] += eights(xf * e)
        dcw_o[32:40, cols] += eights(e0)
        dcw_o[40:48, cols] += eights(grad * grad)
        if c == SUB - 1:
            tail_o[:, cols] = jnp.where(pl.program_id(0) == 0, grad[Q - 8 :, :], tail_o[:, cols])


def edge_kernel(count, ok, piece, *refs):
    ins, piece_o, outs, ext = refs[: 5 * count], refs[5 * count], refs[5 * count + 1 : 6 * count + 1], refs[-1]
    near_o = refs[-2]
    near = jnp.zeros((1, 1), f32)
    piece_o[...] = piece[...]
    group = piece.shape[1] // 2
    for k in range(count):
        tail, rim, cw, xbc, dcw = ins[5 * k : 5 * k + 5]
        dcw_o = outs[k]
        width = tail.shape[1]
        ext[0:8, 0:width] = jnp.zeros((8, width), f32)
        ext[8:16, 0:width] = rim[...]
        last = xbc[...].astype(f32)[8:16]
        grad = tail[...]
        for k8 in range(6):
            dcw_o[k8 : k8 + 1, :] = jnp.sum(dcw[8 * k8 : 8 * k8 + 8, :], axis=0, keepdims=True)
        dcw_o[6:8, :] = jnp.zeros((2, width), f32)
        for j in (1, 2, 3):
            e = ext[j : j + 8, 0:width] * ok[:, j : j + 1]
            grad = grad + cw[3 - j : 4 - j, :] * e
            dcw_o[3 - j : 4 - j, :] += jnp.sum(last * e, axis=0, keepdims=True)
        dcw_o[5:6, :] += jnp.sum(grad * grad, axis=0, keepdims=True)
        near = jnp.maximum(near, jnp.max(dcw_o[5:6, :], axis=1, keepdims=True))
        cols = slice(k * group, k * group + width)
        old = piece[:, cols].astype(f32)
        piece_o[:, cols] = jnp.concatenate([old[0:8], grad], axis=0).astype(bf16)
    near_o[...] = jnp.broadcast_to(near, (8, LANES))


def chain_kernel(backward, pieces, decays, out):
    count, _, width = out.shape

    def turn(i, run):
        k = count - 1 - i if backward else i
        out[k] = run
        return run * decays[k] + pieces[k, :, :width]

    lax.fori_loop(0, count, turn, jnp.zeros(out.shape[1:], f32))


def cost(us):
    return pl.CostEstimate(flops=int(us * 1e9), bytes_accessed=1 << 20, transcendentals=0)


def params(**more):
    return pltpu.CompilerParams(vmem_limit_bytes=VMEM_BYTES, **more)


def to_all(local, lanes):
    count = lax.axis_size("seq")
    rows = local.shape[0]
    if count <= rows:
        got = lax.all_to_all(local.reshape(count, rows // count, lanes + LANES), "seq", 0, 0, tiled=True)
        return got, got[:, 0, lanes:]
    split = count // rows
    got = lax.all_to_all(local[:, :lanes].reshape(count, 1, lanes // split), "seq", 0, 0, tiled=True)
    notes = jnp.broadcast_to(local[0:8, lanes:][None], (count, 8, LANES))
    return got, lax.all_to_all(notes, "seq", 0, 0, tiled=True)[:, 0]


def chain(got, decays, lanes, backward):
    count, per, width = got.shape
    if width > lanes:
        width = lanes
    own = decays[:, None, :]
    if width < lanes:
        split = lanes // width
        own = lax.dynamic_slice_in_dim(own, lax.axis_index("seq") % split * width, width, axis=2)
    out = pl.pallas_call(
        functools.partial(chain_kernel, backward),
        out_shape=jax.ShapeDtypeStruct((count, per, width), f32),
        compiler_params=params(),
    )(got, own)
    return lax.all_to_all(out, "seq", 0, 0, tiled=True).reshape(-1, lanes)


def swap(value, k):
    return lax.ppermute(value, "seq", [(i, i ^ k) for i in range(lax.axis_size("seq"))])


def trade(value):
    return lax.all_to_all(value, "seq", 0, 0, tiled=True)


def sum_all(flat):
    count = lax.axis_size("seq")
    rows = -(-flat.shape[0] // (count * LANES))
    pieces = jnp.pad(flat, (0, count * rows * LANES - flat.shape[0])).reshape(count, rows, LANES)
    mine = jnp.sum(trade(pieces), axis=0)
    return trade(jnp.broadcast_to(mine[None], pieces.shape)).reshape(-1)[: flat.shape[0]]


def sum_all_once(flat):
    count = lax.axis_size("seq")
    wide = flat.reshape(-1, LANES)
    return jnp.sum(trade(jnp.broadcast_to(wide[None], (count,) + wide.shape)), axis=0).reshape(-1)


HALF = jnp.float16
TOP = 32768.0


def tie(*values):
    return lax.optimization_barrier(values)


def chip_scatter(product, cols_mine, cols_other, near, bound, first_bits):
    scale = TOP / jnp.maximum(bound, 1e-30)
    count = lax.axis_size("seq")
    chips = count // 2
    chip = lax.axis_index("seq") // 2
    near = jnp.broadcast_to(jnp.maximum(near, 1e-30), (8, LANES))
    away = swap((product(cols_other) * (TOP / near[0, 0])).astype(HALF), 1).astype(f32)
    acc = (product(cols_mine) + away * (swap(near, 1)[0, 0] * (1.0 / TOP))) * scale
    rows, width = acc.shape
    bits = chips.bit_length() - 1
    acc = acc.reshape((2,) * bits + (rows // chips, width))
    left = list(range(bits))[::-1]
    order = [b for b in first_bits if b < bits]
    order = order + [b for b in range(bits) if b not in order]
    for b in order:
        axis = left.index(b)
        left.remove(b)
        mine = (chip >> b) & 1
        away = lax.dynamic_index_in_dim(acc, 1 - mine, axis, keepdims=False).astype(HALF)
        acc = lax.dynamic_index_in_dim(acc, mine, axis, keepdims=False)
        away, acc = yield away, acc
        arrived = yield swap(away, 2 << b)
        acc = acc + arrived.astype(f32)
    return acc * (1.0 / scale)


class Flow:
    def __init__(self, steps):
        self.steps, self.result = steps, None
        self.value = next(steps)

    def push(self, value):
        try:
            self.value = self.steps.send(value)
        except StopIteration as end:
            self.result = end.value

    def finish(self):
        while self.result is None:
            self.push(self.value)
        return self.result


def beside(flows, operand, kernel):
    flows = [f for f in flows if f.result is None]
    pairs = [f.value for f in flows]
    flat = tie(operand, *[v for p in pairs for v in p])
    for k, f in enumerate(flows):
        f.push((flat[1 + 2 * k], flat[2 + 2 * k]))
    results = kernel(flat[0])
    flat = tie(results[0], *[f.value for f in flows])
    for k, f in enumerate(flows):
        f.push(flat[1 + k])
    return (flat[0],) + tuple(results[1:])


def both_cores(part):
    core = lax.axis_index("seq") % 2
    rows = part.shape[0] // 2
    mine = lax.dynamic_slice_in_dim(part, core * rows, rows, 0)
    other = swap(lax.dynamic_slice_in_dim(part, (1 - core) * rows, rows, 0), 1)
    return jnp.where(core == 0, mine, other), jnp.where(core == 0, other, mine)


def from_behind(value, steps):
    count = lax.axis_size("seq")
    first, last = max(0, -steps), min(count, count - steps)
    return lax.ppermute(value, "seq", [(s, s + steps) for s in range(first, last)])


def body(
    hidden, scene_lengths, norm_gain, w_in, conv_weight, conv_bias, dt_bias, a_log, d_skip,
    gate_gain, w_out, out_grad,
):
    tokens, model = hidden.shape
    heads = a_log.shape[0]
    inner = gate_gain.shape[0]
    channels = conv_bias.shape[0]
    state = (channels - inner) // 2
    chunks = tokens // Q
    repeat = LANES // heads
    columns = w_in.shape[1]

    scenes = scene_lengths.shape[0]
    order = jnp.arange(scenes)
    starts = jnp.sum(jnp.where(order[None, :] < order[:, None], scene_lengths[None, :], 0), axis=1)
    dev_start = lax.axis_index("seq") * tokens
    wide_pos = dev_start + jnp.arange(tokens + 8, dtype=jnp.int32)
    begin_all = jnp.max(jnp.where(starts[None, :] <= wide_pos[:, None], starts[None, :], 0), axis=1)
    begin, pos = begin_all[:tokens], wide_pos[:tokens]
    chunk_last = jnp.repeat(begin.reshape(chunks, Q)[:, -1], Q)
    chunk_start = pos // Q * Q
    inside = jnp.arange(tokens)
    notes = [
        begin,
        pos - 1 >= begin,
        pos - 2 >= begin,
        pos - 3 >= begin,
        (begin_all[1 : tokens + 1] <= pos) & (inside + 1 < tokens),
        (begin_all[2 : tokens + 2] <= pos) & (inside + 2 < tokens),
        (begin_all[3 : tokens + 3] <= pos) & (inside + 3 < tokens),
        begin == chunk_last,
        begin < chunk_start,
        begin < dev_start,
        begin != pos,
    ]
    meta = jnp.stack([n.astype(f32) for n in notes] + [jnp.zeros((tokens,), f32)] * (16 - len(notes)), axis=1)
    brow = begin.astype(f32).reshape(chunks, 1, Q)

    head_of = np.arange(inner) // (inner // heads)
    expand = np.arange(LANES)[:, None] % heads == head_of[None, :]
    expm, red = jnp.asarray(expand, bf16), jnp.asarray(expand.T, bf16)

    def four(v):
        return jnp.tile(v, repeat).reshape(1, LANES)

    gain_row = norm_gain.reshape(1, model)
    w_t = w_in.T
    w_dt = jnp.tile(w_t[inner + channels :], (repeat, 1)).T
    dsk = jnp.repeat(d_skip, inner // heads).reshape(1, inner)
    cb = conv_bias.reshape(1, channels)
    gate_row = gate_gain.reshape(1, inner)

    edge = hidden[tokens - 8 :].astype(f32)
    edge_low = (
        edge * lax.rsqrt(jnp.mean(edge * edge, axis=1, keepdims=True) + EPS) * norm_gain
    ).astype(bf16)
    edge_xbc = jnp.dot(
        edge_low, w_in[:, inner : inner + channels], preferred_element_type=f32
    ).astype(bf16)
    rim = from_behind(edge_xbc, 1).astype(f32)

    tb = SUB * Q
    whole = lambda shape: pl.BlockSpec(shape, lambda i: (0,) * len(shape), pipeline_mode=pl.Buffered(1))
    rowsb = lambda n, width: pl.BlockSpec((n, width), lambda i: (i, 0))
    sds = jax.ShapeDtypeStruct
    (nl, xbc, x, bc, dsil, step, sig, la, cum, decay, sloc, dev_state) = pl.pallas_call(
        functools.partial(project_kernel, heads, inner, state),
        grid=(tokens // tb,),
        in_specs=[
            rowsb(tb, model), whole((8, channels)), whole((1, model)),
            pl.BlockSpec((inner, model), lambda i: (1, 0), pipeline_mode=pl.Buffered(1)),
            pl.BlockSpec((2 * state, model), lambda i: (2 * inner // (2 * state), 0), pipeline_mode=pl.Buffered(1)),
            whole((model, LANES)), whole((4, channels)), whole((1, channels)), whole((1, LANES)),
            whole((1, LANES)), rowsb(tb, 16), whole((LANES, inner)),
        ],
        out_specs=[
            rowsb(tb, model), rowsb(tb, channels), rowsb(tb, inner), rowsb(tb, 2 * state),
            rowsb(tb, channels), rowsb(tb, LANES), rowsb(tb, LANES), rowsb(tb, LANES),
            rowsb(tb // Q * 8, LANES), rowsb(tb // Q * 8, inner),
            pl.BlockSpec((tb // Q, state, inner), lambda i: (i, 0, 0)),
            pl.BlockSpec((state, inner + LANES), lambda i: (0, 0)),
        ],
        out_shape=[
            sds((tokens, model), bf16), sds((tokens, channels), bf16), sds((tokens, inner), f32),
            sds((tokens, 2 * state), f32), sds((tokens, channels), f32), sds((tokens, LANES), f32),
            sds((tokens, LANES), f32), sds((tokens, LANES), f32), sds((chunks * 8, LANES), f32),
            sds((chunks * 8, inner), f32),
            sds((chunks, state, inner), f32), sds((state, inner + LANES), f32),
        ],
        scratch_shapes=[
            pltpu.VMEM((tb + 8, channels), f32), pltpu.VMEM((state, inner), f32), pltpu.VMEM((8, LANES), f32),
            pltpu.VMEM((3, tb, LANES), f32),
        ],
        compiler_params=params(),
        cost_estimate=cost(44),
    )(hidden, rim, gain_row, w_t, w_t, w_dt, conv_weight, cb, four(dt_bias), four(a_log), meta, expm)

    to_lanes = lambda d: jnp.repeat(d[..., :heads], inner // heads, axis=-1)
    got, notes = to_all(dev_state, inner)
    decays = to_lanes(notes)
    state_in = chain(got, decays, inner, False)

    z = jnp.dot(nl, w_in[:, :inner], preferred_element_type=f32)
    yss = pl.pallas_call(
        functools.partial(scan_kernel, heads, inner, state),
        grid=(chunks // SUB,),
        in_specs=[
            rowsb(tb, inner), rowsb(tb, 2 * state), rowsb(tb, LANES), rowsb(tb, LANES), rowsb(tb, 16),
            pl.BlockSpec((SUB, 1, Q), lambda i: (i, 0, 0)),
            pl.BlockSpec((SUB, state, inner), lambda i: (i, 0, 0)), whole((LANES, inner)),
        ],
        out_specs=rowsb(tb, inner),
        out_shape=sds((tokens, inner), f32),
        compiler_params=params(),
        cost_estimate=cost(41),
    )(x, bc, step, la, meta, brow, sloc, expm)

    gate_low, dy, gz, rowdot, state_in_grad, dgain, dskip = pl.pallas_call(
        functools.partial(gate_kernel, heads, inner, state),
        grid=(tokens // tb,),
        in_specs=[
            rowsb(tb, inner), rowsb(tb, inner), rowsb(tb, inner), rowsb(tb, model), whole((inner, model)),
            whole((state, inner)), rowsb(tb, 2 * state), rowsb(tb, LANES), rowsb(8 * SUB, LANES), rowsb(tb, 16),
            whole((1, inner)), whole((1, inner)), whole((LANES, inner)), whole((inner, LANES)),
        ],
        out_specs=[
            rowsb(tb, inner), rowsb(tb, inner), rowsb(tb, inner), rowsb(tb, LANES),
            pl.BlockSpec((state, inner + LANES), lambda i: (0, 0)), pl.BlockSpec((8, inner), lambda i: (0, 0)),
            pl.BlockSpec((8, inner), lambda i: (0, 0)),
        ],
        out_shape=[
            sds((tokens, inner), bf16), sds((tokens, inner), f32), sds((tokens, inner), bf16),
            sds((tokens, LANES), f32), sds((state, inner + LANES), f32), sds((8, inner), f32), sds((8, inner), f32),
        ],
        scratch_shapes=[
            pltpu.VMEM((tb, inner), f32), pltpu.VMEM((tb, inner), f32), pltpu.VMEM((3 * state, inner), bf16),
            pltpu.VMEM((tb, inner), f32), pltpu.VMEM((tb, inner), f32), pltpu.VMEM((8, model), f32),
        ],
        compiler_params=params(),
        cost_estimate=cost(50),
    )(yss, x, z, out_grad, w_out, state_in, bc, la, cum, meta, dsk, gate_row, expm, red)

    got, bounds = to_all(state_in_grad, inner)
    mixed_out = (hidden.astype(f32) + jnp.dot(gate_low, w_out, preferred_element_type=f32)).astype(bf16)
    normed_grad = jnp.einsum("te,de->td", gz, w_in[:, :inner], preferred_element_type=f32)
    state_out_grad = chain(got, decays, inner, True)
    state_out = dev_state[:, :inner] + to_lanes(dev_state[0:1, inner:]) * state_in

    core = lax.axis_index("seq") % 2
    contract = lambda left: lambda right: lax.dot_general(
        left, right, (((0,), (0,)), ((), ())), preferred_element_type=f32
    )
    halfc = inner // 2
    at = lambda v, c: lax.dynamic_slice_in_dim(v, c * halfc, halfc, 1)
    low_most = 1.02 * jnp.sqrt(jnp.float32(inner * tokens)) * jnp.max(jnp.abs(gate_gain))
    nl_most = 1.02 * jnp.sqrt(jnp.float32(model * tokens)) * jnp.max(jnp.abs(norm_gain))
    gz_bounds = jnp.sqrt(bounds[:, 0]) * nl_most
    og_bounds = jnp.sqrt(bounds[:, LANES - 1]) * low_most
    me = lax.axis_index("seq")
    flows = [
        Flow(chip_scatter(contract(out_grad), at(gate_low, core), at(gate_low, 1 - core), og_bounds[me], jnp.sum(og_bounds), (0, 1))),
        Flow(chip_scatter(contract(nl), at(gz, core), at(gz, 1 - core), gz_bounds[me], jnp.sum(gz_bounds), (1, 0))),
    ]

    final = chunks // SUB - 1
    width = 5 * LANES
    full = inner // width
    left_cols = inner - full * width
    conv_left = channels - full * width
    back = lambda n, cols: pl.BlockSpec((n, cols), lambda i: (final - i, 0))
    still = lambda shape: pl.BlockSpec(shape, lambda i: (0,) * len(shape))
    brow_spec = pl.BlockSpec((SUB, 1, Q), lambda i: (final - i, 0, 0))
    acc_specs = [back(tb, 4 * LANES), back(8 * SUB, LANES)]
    acc_shapes = [sds((tokens, 4 * LANES), f32), sds((chunks * 8, LANES), f32)]

    def back_group(g, dsk, acc, into):
        last_one = g == full
        w, wc = (left_cols, conv_left) if last_one else (width, width)
        b, bcv = (full * width // w, full * width // wc)if last_one else (g, g)
        chunk_cols = lambda n: pl.BlockSpec((n, w), lambda i: (final - i, b))
        conv_cols = lambda n: pl.BlockSpec((n, wc), lambda i: (final - i, bcv))
        fixed = lambda n, cols, block: pl.BlockSpec((n, cols), lambda i: (0, block), pipeline_mode=pl.Buffered(1))
        ins = [
            x, bc, step, la, decay, meta, brow, sloc, state_in, dy, dsil, xbc, state_out_grad,
            state_out, dsk, conv_weight, expm, red, *acc,
        ]
        specs = [
            chunk_cols(tb), back(tb, 2 * state), back(tb, LANES), back(tb, LANES), chunk_cols(8 * SUB),
            back(tb, 16), brow_spec, pl.BlockSpec((SUB, state, w), lambda i: (final - i, 0, b)),
            fixed(state, w, b), chunk_cols(tb), conv_cols(tb), conv_cols(tb), fixed(state, w, b),
            fixed(state, w, b), fixed(1, w, b), fixed(4, wc, bcv), fixed(LANES, w, b),
            pl.BlockSpec((w, LANES), lambda i: (b, 0), pipeline_mode=pl.Buffered(1)),
        ] + (acc_specs if acc else [])
        if last_one:
            ins += [sig, rowdot, four(a_log)]
            specs += [back(tb, LANES), back(tb, LANES), still((1, LANES))]
        aliases = {}
        if into is not None:
            aliases[len(ins)] = 0
            ins.append(into)
            specs.append(pl.BlockSpec(memory_space=pl.ANY))
        pg_spec = pl.BlockSpec((tb, width), lambda i: (final - i, g % 2))
        mid_specs, mid_shapes = (
            ([still((8, LANES))], [sds((8, LANES), f32)]) if last_one else (acc_specs, acc_shapes)
        )
        return pl.pallas_call(
            functools.partial(
                back_kernel, heads, inner // heads, state, g * width // (inner // heads), bool(acc),
                into is not None, last_one,
            ),
            grid=(chunks // SUB,),
            in_specs=specs,
            out_specs=[pg_spec] + mid_specs + [still((8, wc)), still((8, wc)), still((48, wc))],
            out_shape=[sds((tokens, 2 * width), bf16)]
            + mid_shapes
            + [sds((8, wc), f32), sds((8, wc), f32), sds((48, wc), f32)],
            scratch_shapes=[
                pltpu.VMEM((state, w), f32), pltpu.VMEM((tb + 8, wc), f32), pltpu.VMEM((8, LANES), f32),
                pltpu.VMEM((3, Q, LANES), f32),
            ],
            input_output_aliases=aliases,
            compiler_params=params(),
            cost_estimate=cost(20 if last_one else 38),
        )(*ins)

    ok_notes = jnp.stack(
        [(begin_all[tokens - 8 + j : tokens + j] <= wide_pos[tokens - 8 : tokens]).astype(f32) for j in range(4)], axis=1
    )

    def fix(part, rims, tails, sums, groups):
        at_last = pl.BlockSpec((16, 2 * width), lambda i: (tokens // 16 - 1, 0))
        ins, specs = [ok_notes, part], [whole((8, 4)), at_last]
        out_specs, shapes = [at_last], [sds(part.shape, bf16)]
        for rim_grad, tail, dcw, g in zip(rims, tails, sums, groups):
            w = tail.shape[1]
            b = g * width // w
            ins += [tail, rim_grad, conv_weight, xbc, dcw]
            specs += [
                whole((8, w)), whole((8, w)), pl.BlockSpec((4, w), lambda i, b=b: (0, b)),
                pl.BlockSpec((16, w), lambda i, b=b: (tokens // 16 - 1, b)), whole((48, w)),
            ]
            out_specs.append(pl.BlockSpec((8, w), lambda i: (0, 0)))
            shapes.append(sds((8, w), f32))
        out_specs.append(pl.BlockSpec((8, LANES), lambda i: (0, 0)))
        shapes.append(sds((8, LANES), f32))
        res = pl.pallas_call(
            functools.partial(edge_kernel, len(groups)), grid=(1,), in_specs=specs, out_specs=out_specs,
            out_shape=shapes, scratch_shapes=[pltpu.VMEM((16, width), f32)], input_output_aliases={1: 0},
            compiler_params=params(),
        )(*ins)
        return res[0], list(res[1:-1]), res[-1]

    reorder2 = lambda r: (r[1], r[0]) + tuple(r[2:])
    reorder = lambda r: (r[2],) + (r[0], r[1]) + tuple(r[3:])
    restore = lambda r: (r[1], r[2], r[0]) + tuple(r[3:])
    parts, rims, tails, sums = [], [], [], []
    acc, into = (), None
    for g in range(full):
        res = beside(flows, dsk, lambda m: reorder(back_group(g, m, acc, into)))
        part, a0, a1, first_g, tail_g, dcw_g = restore(res)
        acc = (a0, a1)
        rims.append(from_behind(first_g, -1))
        tails.append(tail_g)
        sums.append(dcw_g)
        into = part if g % 2 == 0 else None
        if g % 2 == 1:
            parts.append(part)
    part_a, dcws, near_a = fix(parts[0], rims[0:2], tails[0:2], sums[0:2], (0, 1))

    def bound_of(near):
        near = jnp.sqrt(near) * nl_most
        return near[0, 0], jnp.sum(trade(jnp.broadcast_to(near, (lax.axis_size("seq"), 8, LANES)))[:, 0, 0])

    own = lambda v, c: lax.dynamic_slice_in_dim(v, c * width, width, 1)
    flow_a = Flow(
        chip_scatter(contract(nl), own(part_a, core), own(part_a, 1 - core), *bound_of(near_a), (0, 1))
    )
    flows.append(flow_a)
    res = beside(flows, dsk, lambda m: reorder2(back_group(full, m, acc, into)))
    small, part, first_g, tail_g, dcw_g = res
    rims.append(from_behind(first_g, -1))
    part_b, dcw_b, near_b = fix(part, rims[2:], tails[2:] + [tail_g], sums[2:] + [dcw_g], (2, 3))
    bound_b = bound_of(jnp.maximum(near_b, jnp.max(small[2])))
    flow_b = Flow(
        chip_scatter(contract(nl), own(part_b, core), own(part_b, 1 - core), *bound_b, (1, 0))
    )
    dcw = jnp.concatenate(dcws + dcw_b, axis=1)

    (away, kept) = flow_b.value
    part_a2, part_b2, dcw, small, out_done, z_done, a_away, a_kept, away, kept = tie(
        part_a, part_b, dcw, small, flows[0].finish(), flows[1].finish(), *flow_a.value, away, kept
    )
    flow_a.push((a_away, a_kept))
    conv_weight_part = dcw[0:4]
    flow_b.push((away, kept))
    cut = inner + 2 * width
    normed_grad = (
        normed_grad
        + jnp.dot(part_a2, w_t[inner:cut], preferred_element_type=f32)
        + jnp.dot(part_b2[:, : columns - cut], w_t[cut:], preferred_element_type=f32)
    )
    out_rows = jnp.concatenate(both_cores(out_done), axis=1)
    w_out_grad = out_rows.T
    z_rows = both_cores(z_done)
    a_rows = both_cores(flow_a.finish())
    b_rows = both_cores(flow_b.finish())
    w_in_grad = jnp.concatenate(list(z_rows) + list(a_rows) + list(b_rows), axis=1)[:, :columns]

    hv = hidden.astype(f32)
    s = lax.rsqrt(jnp.mean(hv * hv, axis=1, keepdims=True) + EPS)
    gained = normed_grad * norm_gain
    inner_mean = jnp.mean(gained * hv, axis=1, keepdims=True)
    hidden_grad = out_grad.astype(f32) + s * gained - hv * (s * s * s * inner_mean)
    norm_gain_part = jnp.sum(normed_grad * hv * s, axis=0)

    dskip_part = jnp.sum(dskip[0].reshape(heads, inner // heads), axis=1)
    early = (conv_weight_part.reshape(-1), dcw[4], small[1, :heads], small[0, :heads], dskip_part, dgain[0])
    total = sum_all(jnp.concatenate(early))
    summed, start = [], 0
    for part in early:
        summed.append(total[start : start + part.shape[0]])
        start += part.shape[0]
    norm_gain_grad = sum_all_once(norm_gain_part)
    return (
        mixed_out, hidden_grad, norm_gain_grad, w_in_grad, summed[0].reshape(conv_weight.shape), summed[1],
        summed[2], summed[3], summed[4], summed[5], w_out_grad,
    )


def solution(mesh):
    rep = P()
    return jax.shard_map(
        body,
        mesh=mesh,
        in_specs=(P("seq", None),) + (rep,) * 10 + (P("seq", None),),
        out_specs=(P("seq", None), P("seq", None), rep, P("seq", None), rep, rep, rep, rep, rep, rep, P(None, "seq")),
        check_vma=False,
    )
```

```python
import functools

import jax
import jax.numpy as jnp
import numpy as np
from jax import lax
from jax.experimental import pallas as pl
from jax.experimental.pallas import tpu as pltpu
from jax.sharding import PartitionSpec as P

Q = 128
LANES = 128
EPS = 1e-05
LOG2E = 1.4426950408889634
f32 = jnp.float32
bf16 = jnp.bfloat16
VMEM_BYTES = 60 << 20
SUB = 2
WIDE = 256


def mm(a, b):
    return lax.dot_general(a, b, (((1,), (0,)), ((), ())), preferred_element_type=f32)


def mm_nt(a, b):
    return lax.dot_general(a, b, (((1,), (1,)), ((), ())), preferred_element_type=f32)


def mm_tn(a, b):
    return lax.dot_general(a, b, (((0,), (0,)), ((), ())), preferred_element_type=f32)


def split2(v):
    hi = v.astype(bf16)
    return hi, (v - hi.astype(f32)).astype(bf16)


def sigmoid(v):
    return jax.nn.sigmoid(v)


def lane_iota(rows):
    return lax.broadcasted_iota(jnp.int32, (rows, LANES), 1)


def spread(v, heads):
    hi = v.astype(bf16).astype(f32)
    rest = v - hi
    mid = rest.astype(bf16).astype(f32)
    low = rest - mid
    lane = lane_iota(v.shape[0])
    kept = jnp.where(lane < heads, hi, jnp.where(lane < 2 * heads, mid, low))
    return jnp.where(lane < 3 * heads, kept, 0.0).astype(bf16)


def exact3(v):
    hi = v.astype(bf16)
    rest = v - hi.astype(f32)
    mid = rest.astype(bf16)
    return hi, mid, (rest - mid.astype(f32)).astype(bf16)


def mask_mm(mask, v):
    hi, mid, low = exact3(v)
    return mm(mask, hi) + mm(mask, mid) + mm(mask, low)


def prod3(a_hi, a_lo, b_hi, b_lo):
    left = jnp.concatenate([a_hi, a_lo], axis=1)
    return mm(left, jnp.concatenate([b_hi, b_hi], axis=0)) + mm(a_hi, b_lo)


def head_sums(v, red):
    hi, lo = split2(v)
    return mm(hi, red) + mm(lo, red)


def tri_masks(begin_col, begin_row):
    row = lax.broadcasted_iota(jnp.int32, (Q, Q), 0)
    col = lax.broadcasted_iota(jnp.int32, (Q, Q), 1)
    same = jnp.broadcast_to(begin_col, (Q, Q)) == jnp.broadcast_to(begin_row, (Q, Q))
    return same & (row >= col), same & (row <= col)


def project_kernel(
    heads, inner, state,
    hid, rim, gain, w_x, w_bc, w_dt, cw, cb, dtb, alog, meta, expm,
    nl_o, xbc_o, x_o, bc_o, dsil_o, step_o, sig_o, la_o, cum_o, decay_o, sloc_o, dst_o,
    ext, srun, cum, msk,
):
    rows = hid.shape[0]
    channels = inner + 2 * state
    step_id = pl.program_id(0)

    @pl.when(step_id == 0)
    def _():
        ext[0:8, :] = rim[...]
        srun[...] = jnp.zeros_like(srun)
        cum[...] = jnp.zeros_like(cum)

    hv = hid[...].astype(f32)
    mean = jnp.mean(hv * hv, axis=1, keepdims=True)
    nl = (hv * lax.rsqrt(mean + EPS) * gain[...]).astype(bf16)
    nl_o[...] = nl

    v = mm(nl, w_dt[...]) + dtb[...]
    step = jnp.maximum(v, 0.0) + jnp.log1p(jnp.exp(-jnp.abs(v)))
    step_o[...] = step
    sig_o[...] = 1.0 / (1.0 + jnp.exp(-v))
    rate = -step * (jnp.exp(alog[...]) * LOG2E)

    for j in range(3):
        msk[j] = jnp.broadcast_to(meta[:, 1 + j : 2 + j], (rows, LANES))
    m1, m2, m3 = (jnp.concatenate([msk[j]] * (WIDE // LANES), axis=1) for j in range(3))
    for g in range(channels // WIDE):
        cols = slice(g * WIDE, (g + 1) * WIDE)
        weights = w_x[cols, :] if g * WIDE < inner else w_bc[...]
        low = mm_nt(nl, weights).astype(bf16)
        xbc_o[:, cols] = low
        ext[8 : 8 + rows, cols] = low.astype(f32)
        conv = cb[:, cols] + cw[3:4, cols] * ext[8 : 8 + rows, cols]
        conv = conv + cw[2:3, cols] * (ext[7 : 7 + rows, cols] * m1)
        conv = conv + cw[1:2, cols] * (ext[6 : 6 + rows, cols] * m2)
        conv = conv + cw[0:1, cols] * (ext[5 : 5 + rows, cols] * m3)
        gate = sigmoid(conv)
        act = conv * gate
        dsil_o[:, cols] = gate + act * (1.0 - gate)
        if g * WIDE < inner:
            x_o[:, cols] = act
        else:
            bc_o[...] = act
    ext[0:8, :] = ext[rows : rows + 8, :]

    row = lax.broadcasted_iota(jnp.int32, (Q, Q), 0)
    col = lax.broadcasted_iota(jnp.int32, (Q, Q), 1)
    tri = (row >= col).astype(bf16)
    for c in range(rows // Q):
        rs = slice(c * Q, (c + 1) * Q)
        la = mask_mm(tri, rate[rs])
        la_o[rs, :] = la
        enter = jnp.exp2(cum[...]) * meta[c * Q : c * Q + 1, 9:10]
        cum_o[c * 8 : (c + 1) * 8, :] = cum[...]
        last = la[Q - 1 : Q, :]
        cum[...] = cum[...] + last
        weight = jnp.exp2(last - la) * meta[rs, 7:8] * step[rs]
        decay = jnp.exp2(last) * meta[c * Q + Q - 1 : c * Q + Q, 8:9]
        sub = lax.broadcasted_iota(jnp.int32, (8, LANES), 0)
        both = jnp.where(sub == 0, jnp.broadcast_to(decay, (8, LANES)), enter)
        factors = jnp.concatenate([spread(weight, heads), spread(both, heads), jnp.zeros((8, LANES), bf16)], axis=0)
        b_t = bc_o[rs, :state].T
        bt_hi, bt_lo = split2(b_t)
        for g in range(inner // WIDE):
            cols = slice(g * WIDE, (g + 1) * WIDE)
            wide = mm(factors, expm[:, cols])
            decay_o[c * 8 : (c + 1) * 8, cols] = wide[Q : Q + 8]
            hi, lo = split2(x_o[rs, cols] * wide[:Q])
            new = prod3(bt_hi, bt_lo, hi, lo)
            old = srun[:, cols]
            sloc_o[c, :, cols] = old
            srun[:, cols] = old * wide[Q : Q + 1] + new
        if c == rows // Q - 1:
            @pl.when(step_id == pl.num_programs(0) - 1)
            def _():
                live = meta[c * Q + Q - 1 : c * Q + Q, 9:10]
                total = jnp.exp2(cum[...]) * live
                dst_o[:, :inner] = srun[...]
                dst_o[:, inner:] = jnp.broadcast_to(total[0:1], (state, LANES))


def over_heads(v, first, count, half):
    shape = (v.shape[0], LANES)
    column = lambda h: jnp.broadcast_to(v[:, h : h + 1], shape)
    pairs = [jnp.where(half, column(h), column(h + 1)) for h in range(first, first + count, 2)]
    return jnp.concatenate(pairs, axis=1)


def scan_kernel(heads, inner, state, x_r, bc_r, step_r, la_rows, meta_r, brow, sloc, expm, y_o):
    left_half = lane_iota(Q) < inner // heads
    for c in range(SUB):
        rs = slice(c * Q, (c + 1) * Q)
        la = la_rows[rs, :]
        la_t = la.T
        meta, step = meta_r[rs, :], step_r[rs, :]
        mask, _ = tri_masks(meta[:, 0:1], brow[c])
        b_hi, b_lo = split2(bc_r[rs, :state])
        c_hi, c_lo = split2(bc_r[rs, state:])
        c_cat = jnp.concatenate([c_hi, c_lo], axis=1)
        scores = mm_nt(c_cat, jnp.concatenate([b_hi, b_hi], axis=1)) + mm_nt(c_hi, b_lo)
        scores = jnp.where(mask, scores, 0.0)
        carry_s = spread(jnp.exp2(la) * meta[:, 8:9], heads)
        for k in range(inner // WIDE):
            wide_cols = slice(k * WIDE, (k + 1) * WIDE)
            first = k * WIDE * heads // inner
            s_hi, s_lo = split2(sloc[c, :, wide_cols])
            carried = mm(carry_s, expm[:, wide_cols]) * (
                mm(c_cat, jnp.concatenate([s_hi, s_hi], axis=0)) + mm(c_hi, s_lo)
            )
            step_x = over_heads(step, first, WIDE * heads // inner, left_half)
            all_hi, all_lo = split2(x_r[rs, wide_cols] * step_x)
            for p in range(WIDE // LANES):
                own = slice(p * LANES, (p + 1) * LANES)
                cols = slice(k * WIDE + p * LANES, k * WIDE + (p + 1) * LANES)
                u_cat = jnp.concatenate([all_hi[:, own], all_lo[:, own]], axis=1)
                right = jnp.concatenate([u_cat, u_cat], axis=0)
                lefts = []
                for e in range(2):
                    h = first + 2 * p + e
                    gap = jnp.minimum(la[:, h : h + 1] - la_t[h : h + 1, :], 0.0)
                    w_hi, w_lo = split2(scores * jnp.exp2(gap))
                    lefts.append(jnp.concatenate([w_hi, w_lo], axis=1))
                both = mm(jnp.concatenate(lefts, axis=0), right)
                both = both[:, :LANES] + both[:, LANES:]
                y_o[rs, cols] = jnp.where(left_half, both[:Q], both[Q:]) + carried[:, own]


def gate_kernel(
    heads, inner, state,
    yss, x, z, og, w_out, s_in, bc, la_r, cum, meta, dsk, gain, expm, red,
    gl_o, dy_o, gz_o, rowdot_o, sin_o, dgain_o, dskip_o,
    gsc, ysc, ssc, exs, grad, ogs,
):
    step_id = pl.program_id(0)
    rows = x.shape[0]

    @pl.when(step_id == 0)
    def _():
        sin_o[:, :inner] = jnp.zeros((state, inner), f32)
        dgain_o[...] = jnp.zeros_like(dgain_o)
        dskip_o[...] = jnp.zeros_like(dskip_o)
        ogs[...] = jnp.zeros_like(ogs)
        hi, lo = split2(s_in[...])
        ssc[0:state, :] = hi
        ssc[state : 2 * state, :] = hi
        ssc[2 * state :, :] = lo

    c_hi, c_lo = split2(bc[:, state:])
    c_cat = jnp.concatenate([c_hi, c_lo], axis=1)
    ct_hi, ct_lo = split2(bc[:, state:].T)
    before = jnp.concatenate(
        [jnp.broadcast_to(cum[8 * c : 8 * c + 1, :], (Q, LANES)) for c in range(rows // Q)], axis=0
    )
    enter_s = spread(jnp.exp2(la_r[...] + before) * meta[:, 9:10], heads)
    ogv = og[...]
    ogs[...] += eights(jnp.square(ogv.astype(f32)))
    sq = jnp.zeros((rows, LANES), f32)
    dotted = jnp.zeros((rows, LANES), f32)
    for g in range(inner // WIDE):
        cols = slice(g * WIDE, (g + 1) * WIDE)
        carried = mm(c_cat, ssc[0 : 2 * state, cols]) + mm(c_hi, ssc[2 * state :, cols])
        enter_x = mm(enter_s, expm[:, cols])
        exs[:, cols] = enter_x
        y = yss[:, cols] + carried * enter_x
        ysc[:, cols] = y
        zv = z[:, cols]
        gated = (y + dsk[:, cols] * x[:, cols]) * (zv * sigmoid(zv))
        gsc[:, cols] = gated
        s = gated * gated
        gg = mm_nt(ogv, w_out[cols, :])
        grad[:, cols] = gg
        d = gg * gain[:, cols] * gated
        for k in range(WIDE // LANES):
            sq = sq + s[:, k * LANES : (k + 1) * LANES]
            dotted = dotted + d[:, k * LANES : (k + 1) * LANES]
    mean = jnp.sum(sq, axis=1, keepdims=True) / inner
    r = lax.rsqrt(mean + EPS)
    m = jnp.sum(dotted, axis=1, keepdims=True) / inner
    coeff = r * r * r * m
    rowdot = jnp.zeros((2 * rows, LANES), f32)
    for g in range(inner // WIDE):
        cols = slice(g * WIDE, (g + 1) * WIDE)
        gated = gsc[:, cols]
        gg = grad[:, cols]
        gn = gated * r
        gl_o[:, cols] = (gn * gain[:, cols]).astype(bf16)
        dgain_o[0:1, cols] += jnp.sum(gg * gn, axis=0, keepdims=True)
        grad_gated = r * (gain[:, cols] * gg) - gated * coeff
        zv = z[:, cols]
        sg = sigmoid(zv)
        sz = zv * sg
        dy = grad_gated * sz
        dy_o[:, cols] = dy
        ys = ysc[:, cols]
        xv = x[:, cols]
        gz = grad_gated * (ys + dsk[:, cols] * xv) * (sg + sz * (1.0 - sg))
        gz_o[:, cols] = gz.astype(bf16)
        dgain_o[1:2, cols] += jnp.sum(gz * gz, axis=0, keepdims=True)
        rowdot = rowdot + mm(jnp.concatenate(split2(dy * ys), axis=0), red[cols, :])
        dskip_o[0:1, cols] += jnp.sum(dy * xv, axis=0, keepdims=True)
        hi, lo = split2(dy * exs[:, cols])
        sin_o[:, cols] += mm(ct_hi, hi) + mm(ct_lo, hi) + mm(ct_hi, lo)
    rowdot_o[...] = rowdot[:rows] + rowdot[rows:]

    @pl.when(step_id == pl.num_programs(0) - 1)
    def _():
        most = jnp.max(dgain_o[1:2, :], axis=1, keepdims=True)
        og_most = jnp.max(jnp.sum(ogs[...], axis=0, keepdims=True), axis=1, keepdims=True)
        sin_o[:, inner:] = jnp.where(lane_iota(state) < LANES // 2, most, og_most)


def back_kernel(
    heads, head_width, state, first_head, started, into, last_one,
    x, bc, step_r, la_r, decay, meta, brow, sloc, s_in, dyr, dsil, xbc,
    d_in, s_out, dsk, cw, expm, red, *rest,
):
    if started:
        acc_in, rest = rest[:2], rest[2:]
    if last_one:
        (sig, rowdot, alog), rest = rest[:3], rest[3:]
    if into:
        rest = rest[1:]
    if last_one:
        pg_o, par_o, first_o, tail_o, dcw_o, ds, cgx, tot, msk = rest
    else:
        pg_o, dcb_o, small_o, first_o, tail_o, dcw_o, ds, cgx, tot, msk = rest
    step_id = pl.program_id(0)
    width = x.shape[1]
    rows = SUB * Q

    @pl.when(step_id == 0)
    def _():
        ds[...] = d_in[...]
        cgx[0:8, :] = jnp.zeros_like(cgx[0:8, :])
        dcw_o[...] = jnp.zeros_like(dcw_o)
        if last_one:
            par_o[...] = jnp.zeros_like(par_o)
        for p in range(width // LANES):
            cols = slice(p * LANES, (p + 1) * LANES)
            tot[p : p + 1, :] = jnp.sum(d_in[:, cols] * s_out[:, cols], axis=0, keepdims=True)

    cgx[rows:, :] = cgx[0:8, :]
    pairs = width // LANES
    left_half = lane_iota(Q) < head_width
    zero = jnp.zeros((Q, LANES), bf16)
    lane8 = lane_iota(8)
    pair8 = lax.broadcasted_iota(jnp.int32, (8, LANES), 0)
    for c in reversed(range(SUB)):
        rs = slice(c * Q, (c + 1) * Q)
        part = tot[0:8, :]
        halves = [
            jnp.sum(jnp.where(side, part, 0.0), axis=1, keepdims=True)
            for side in (lane8 < head_width, lane8 >= head_width)
        ]
        ends = jnp.zeros((8, LANES), f32)
        for e in range(2):
            here = (lane8 % heads == first_head + 2 * pair8 + e) & (pair8 < pairs)
            ends = ends + jnp.where(here, halves[e], 0.0)
        ends = jnp.sum(ends, axis=0, keepdims=True)

        la = la_r[rs, :]
        la_t = la.T
        notes = meta[rs, :]
        for j in range(3):
            msk[j] = jnp.broadcast_to(notes[:, 4 + j : 5 + j], (Q, LANES))
        _, mask_t = tri_masks(notes[:, 0:1], brow[c])
        b_hi, b_lo = split2(bc[rs, :state])
        c32 = bc[rs, state:]
        c_hi, c_lo = split2(c32)
        b_cat = jnp.concatenate([b_hi, b_lo], axis=1)
        ct_hi, ct_lo = split2(c32.T)
        scores_t = mm_nt(b_cat, jnp.concatenate([c_hi, c_hi], axis=1)) + mm_nt(b_hi, c_lo)
        scores_t = jnp.where(mask_t, scores_t, 0.0)
        last = la[Q - 1 : Q, :]
        tail = notes[:, 7:8]
        step = step_r[rs, :]
        tail_v = jnp.exp2(last - la) * tail
        factors = jnp.concatenate(
            [spread(step, heads), spread(jnp.exp2(la) * notes[:, 8:9], heads)], axis=0
        )

        dg_t = jnp.zeros((Q, Q), f32)
        dc = jnp.zeros((Q, state), f32)
        db = jnp.zeros((Q, state), f32)
        xdu = jnp.zeros((Q, LANES), f32)
        for lo_col in range(0, width, WIDE):
            wd = min(WIDE, width - lo_col)
            wcols = slice(lo_col, lo_col + wd)
            first = first_head + lo_col // head_width
            wide = mm(factors, expm[:, wcols])
            step_x, carry_x = wide[:Q], wide[Q:]
            tail_x = over_heads(tail_v, first, wd // head_width, left_half)
            xv = x[rs, wcols]
            dy = dyr[rs, wcols]
            u = xv * step_x
            u_hi, u_lo = split2(u)
            dy_hi, dy_lo = split2(dy)
            d_out = ds[:, wcols]
            d_hi, d_lo = split2(d_out)
            through = tail_x * (mm(b_cat, jnp.concatenate([d_hi, d_hi], axis=0)) + mm(b_hi, d_lo))
            insides = []
            for p in range(wd // LANES):
                own = slice(p * LANES, (p + 1) * LANES)
                uh, ul, yh, yl = u_hi[:, own], u_lo[:, own], dy_hi[:, own], dy_lo[:, own]
                sides = []
                for e in range(2):
                    keep = left_half if e == 0 else ~left_half
                    sides.append(
                        jnp.concatenate([jnp.where(keep, uh, zero), jnp.where(keep, ul, zero)], axis=1)
                    )
                right = jnp.concatenate(
                    [jnp.concatenate([yh, yh], axis=1), jnp.concatenate([yl, yl], axis=1)], axis=0
                )
                dw = mm_nt(jnp.concatenate(sides, axis=0), right)
                dw = dw[:, :Q] + dw[:, Q:]
                lefts = []
                for e in range(2):
                    h = first + 2 * p + e
                    gap = jnp.minimum(la_t[h : h + 1, :] - la[:, h : h + 1], 0.0)
                    decays = jnp.exp2(gap)
                    w_hi, w_lo = split2(scores_t * decays)
                    lefts.append(jnp.concatenate([w_hi, w_lo], axis=1))
                    dg_t = dg_t + dw[e * Q : (e + 1) * Q] * decays
                y_cat = jnp.concatenate([yh, yl], axis=1)
                both = mm(jnp.concatenate(lefts, axis=0), jnp.concatenate([y_cat, y_cat], axis=0))
                both = both[:, :LANES] + both[:, LANES:]
                insides.append(jnp.where(left_half, both[:Q], both[Q:]))
            du = through + (jnp.concatenate(insides, axis=1) if len(insides) > 1 else insides[0])
            sums = mm(jnp.concatenate(split2(xv * du), axis=0), red[wcols, :])
            xdu = xdu + sums[:Q] + sums[Q:]
            cgx[rs, wcols] = (dsk[:, wcols] * dy + step_x * du) * dsil[rs, wcols]
            s_true = sloc[c, :, wcols] + decay[8 * c + 1 : 8 * c + 2, wcols] * s_in[:, wcols]
            s_hi, s_lo = split2(s_true)
            v_hi, v_lo = split2(carry_x * dy)
            t_hi, t_lo = split2(tail_x * u)
            res = mm_nt(jnp.concatenate([v_hi, v_lo], axis=0), jnp.concatenate([s_hi, s_lo], axis=0))
            dc = dc + (res[:Q, :state] + res[:Q, state:] + res[Q:, :state])
            res = mm_nt(jnp.concatenate([t_hi, t_lo], axis=0), jnp.concatenate([d_hi, d_lo], axis=0))
            db = db + (res[:Q, :state] + res[:Q, state:] + res[Q:, :state])
            d_new = d_out * decay[8 * c : 8 * c + 1, wcols] + prod3(ct_hi, ct_lo, v_hi, v_lo)
            ds[:, wcols] = d_new
            total = jnp.sum(d_new * s_true, axis=0, keepdims=True)
            for p in range(wd // LANES):
                row = lo_col // LANES + p
                tot[row : row + 1, :] = total[:, p * LANES : (p + 1) * LANES]
            conv_back(c, wcols, msk, cgx, cw, xbc, pg_o, dcw_o, tail_o)

        parts = [dg_t, dc, db, xdu]
        if started:
            parts = [v + acc_in[0][rs, i * LANES : (i + 1) * LANES] for i, v in enumerate(parts)]
            ends = ends + acc_in[1][8 * c : 8 * c + 1, :]
        if not last_one:
            for i, value in enumerate(parts):
                dcb_o[rs, i * LANES : (i + 1) * LANES] = value
            small_o[8 * c : 8 * c + 8, :] = jnp.broadcast_to(ends, (8, LANES))
            continue
        dg_t, dc, db, xdu = parts
        g_hi, g_lo = split2(jnp.where(mask_t, dg_t, 0.0))
        dc = dc + mm_tn(g_hi, b_hi) + mm_tn(g_lo, b_hi) + mm_tn(g_hi, b_lo)
        db = db + mm(g_hi, c_hi) + mm(g_lo, c_hi) + mm(g_hi, c_lo)
        cgx[rs, width : width + state] = db * dsil[rs, width : width + state]
        cgx[rs, width + state :] = dc * dsil[rs, width + state :]
        flow = rowdot[rs, :] - step * xdu
        g = mask_mm(mask_t.astype(bf16), flow) + tail * ends
        g = g * notes[:, 10:11]
        rate = jnp.exp(alog[...])
        dt = (xdu - g * rate) * sig[rs, :]
        used = cgx.shape[1]
        pg_o[rs, used : used + LANES] = jnp.where(lane_iota(Q) < heads, dt, 0.0).astype(bf16)
        pg_o[rs, used + LANES :] = jnp.zeros((Q, pg_o.shape[1] - used - LANES), bf16)
        par_o[0:1, :] += jnp.sum(-g * step * rate, axis=0, keepdims=True)
        par_o[1:2, :] += jnp.sum(dt, axis=0, keepdims=True)
        par_o[2:3, :] += jnp.sum(dt * dt, axis=0, keepdims=True)
        conv_back(c, slice(width, width + 2 * state), msk, cgx, cw, xbc, pg_o, dcw_o, tail_o)
    first_o[...] = cgx[0:8, :]


def eights(v):
    return jnp.sum(v.reshape(v.shape[0] // 8, 8, v.shape[1]), axis=0)


def conv_back(c, which, msk, cgx, cw, xbc, pg_o, dcw_o, tail_o):
    at = c * Q
    for start in range(which.start, which.stop, LANES):
        cols = slice(start, start + LANES)
        e0 = cgx[at : at + Q, cols]
        e1 = cgx[at + 1 : at + Q + 1, cols] * msk[0]
        e2 = cgx[at + 2 : at + Q + 2, cols] * msk[1]
        e3 = cgx[at + 3 : at + Q + 3, cols] * msk[2]
        grad = cw[3:4, cols] * e0 + cw[2:3, cols] * e1 + cw[1:2, cols] * e2 + cw[0:1, cols] * e3
        pg_o[at : at + Q, cols] = grad.astype(bf16)
        xf = xbc[at : at + Q, cols].astype(f32)
        for tap, e in ((3, e0), (2, e1), (1, e2), (0, e3)):
            dcw_o[8 * tap : 8 * tap + 8, cols] += eights(xf * e)
        dcw_o[32:40, cols] += eights(e0)
        dcw_o[40:48, cols] += eights(grad * grad)
        if c == SUB - 1:
            tail_o[:, cols] = jnp.where(pl.program_id(0) == 0, grad[Q - 8 :, :], tail_o[:, cols])


def edge_kernel(count, ok, piece, *refs):
    ins, piece_o, outs, ext = refs[: 5 * count], refs[5 * count], refs[5 * count + 1 : 6 * count + 1], refs[-1]
    near_o = refs[-2]
    near = jnp.zeros((1, 1), f32)
    piece_o[...] = piece[...]
    group = piece.shape[1] // 2
    for k in range(count):
        tail, rim, cw, xbc, dcw = ins[5 * k : 5 * k + 5]
        dcw_o = outs[k]
        width = tail.shape[1]
        ext[0:8, 0:width] = jnp.zeros((8, width), f32)
        ext[8:16, 0:width] = rim[...]
        last = xbc[...].astype(f32)[8:16]
        grad = tail[...]
        for k8 in range(6):
            dcw_o[k8 : k8 + 1, :] = jnp.sum(dcw[8 * k8 : 8 * k8 + 8, :], axis=0, keepdims=True)
        dcw_o[6:8, :] = jnp.zeros((2, width), f32)
        for j in (1, 2, 3):
            e = ext[j : j + 8, 0:width] * ok[:, j : j + 1]
            grad = grad + cw[3 - j : 4 - j, :] * e
            dcw_o[3 - j : 4 - j, :] += jnp.sum(last * e, axis=0, keepdims=True)
        dcw_o[5:6, :] += jnp.sum(grad * grad, axis=0, keepdims=True)
        near = jnp.maximum(near, jnp.max(dcw_o[5:6, :], axis=1, keepdims=True))
        cols = slice(k * group, k * group + width)
        old = piece[:, cols].astype(f32)
        piece_o[:, cols] = jnp.concatenate([old[0:8], grad], axis=0).astype(bf16)
    near_o[...] = jnp.broadcast_to(near, (8, LANES))


def chain_kernel(backward, pieces, decays, out):
    count, _, width = out.shape

    def turn(i, run):
        k = count - 1 - i if backward else i
        out[k] = run
        return run * decays[k] + pieces[k, :, :width]

    lax.fori_loop(0, count, turn, jnp.zeros(out.shape[1:], f32))


def cost(us):
    return pl.CostEstimate(flops=int(us * 1e9), bytes_accessed=1 << 20, transcendentals=0)


def params(**more):
    return pltpu.CompilerParams(vmem_limit_bytes=VMEM_BYTES, **more)


def to_all(local, lanes):
    count = lax.axis_size("seq")
    rows = local.shape[0]
    if count <= rows:
        got = lax.all_to_all(local.reshape(count, rows // count, lanes + LANES), "seq", 0, 0, tiled=True)
        return got, got[:, 0, lanes:]
    split = count // rows
    got = lax.all_to_all(local[:, :lanes].reshape(count, 1, lanes // split), "seq", 0, 0, tiled=True)
    notes = jnp.broadcast_to(local[0:8, lanes:][None], (count, 8, LANES))
    return got, lax.all_to_all(notes, "seq", 0, 0, tiled=True)[:, 0]


def chain(got, decays, lanes, backward):
    count, per, width = got.shape
    if width > lanes:
        width = lanes
    own = decays[:, None, :]
    if width < lanes:
        split = lanes // width
        own = lax.dynamic_slice_in_dim(own, lax.axis_index("seq") % split * width, width, axis=2)
    out = pl.pallas_call(
        functools.partial(chain_kernel, backward),
        out_shape=jax.ShapeDtypeStruct((count, per, width), f32),
        compiler_params=params(),
    )(got, own)
    return lax.all_to_all(out, "seq", 0, 0, tiled=True).reshape(-1, lanes)


def swap(value, k):
    return lax.ppermute(value, "seq", [(i, i ^ k) for i in range(lax.axis_size("seq"))])


def trade(value):
    return lax.all_to_all(value, "seq", 0, 0, tiled=True)


def sum_all(flat):
    count = lax.axis_size("seq")
    rows = -(-flat.shape[0] // (count * LANES))
    pieces = jnp.pad(flat, (0, count * rows * LANES - flat.shape[0])).reshape(count, rows, LANES)
    mine = jnp.sum(trade(pieces), axis=0)
    return trade(jnp.broadcast_to(mine[None], pieces.shape)).reshape(-1)[: flat.shape[0]]


def sum_all_once(flat):
    count = lax.axis_size("seq")
    wide = flat.reshape(-1, LANES)
    return jnp.sum(trade(jnp.broadcast_to(wide[None], (count,) + wide.shape)), axis=0).reshape(-1)


HALF = jnp.float16
TOP = 32768.0


def tie(*values):
    return lax.optimization_barrier(values)


def chip_scatter(product, cols_mine, cols_other, near, bound, first_bits):
    scale = TOP / jnp.maximum(bound, 1e-30)
    count = lax.axis_size("seq")
    chips = count // 2
    chip = lax.axis_index("seq") // 2
    near = jnp.broadcast_to(jnp.maximum(near, 1e-30), (8, LANES))
    away = swap((product(cols_other) * (TOP / near[0, 0])).astype(HALF), 1).astype(f32)
    acc = (product(cols_mine) + away * (swap(near, 1)[0, 0] * (1.0 / TOP))) * scale
    rows, width = acc.shape
    bits = chips.bit_length() - 1
    acc = acc.reshape((2,) * bits + (rows // chips, width))
    left = list(range(bits))[::-1]
    order = [b for b in first_bits if b < bits]
    order = order + [b for b in range(bits) if b not in order]
    for b in order:
        axis = left.index(b)
        left.remove(b)
        mine = (chip >> b) & 1
        away = lax.dynamic_index_in_dim(acc, 1 - mine, axis, keepdims=False).astype(HALF)
        acc = lax.dynamic_index_in_dim(acc, mine, axis, keepdims=False)
        away, acc = yield away, acc
        arrived = yield swap(away, 2 << b)
        acc = acc + arrived.astype(f32)
    return acc * (1.0 / scale)


class Flow:
    def __init__(self, steps):
        self.steps, self.result = steps, None
        self.value = next(steps)

    def push(self, value):
        try:
            self.value = self.steps.send(value)
        except StopIteration as end:
            self.result = end.value

    def finish(self):
        while self.result is None:
            self.push(self.value)
        return self.result


def beside(flows, operand, kernel):
    flows = [f for f in flows if f.result is None]
    pairs = [f.value for f in flows]
    flat = tie(operand, *[v for p in pairs for v in p])
    for k, f in enumerate(flows):
        f.push((flat[1 + 2 * k], flat[2 + 2 * k]))
    results = kernel(flat[0])
    flat = tie(results[0], *[f.value for f in flows])
    for k, f in enumerate(flows):
        f.push(flat[1 + k])
    return (flat[0],) + tuple(results[1:])


def both_cores(part):
    core = lax.axis_index("seq") % 2
    rows = part.shape[0] // 2
    mine = lax.dynamic_slice_in_dim(part, core * rows, rows, 0)
    other = swap(lax.dynamic_slice_in_dim(part, (1 - core) * rows, rows, 0), 1)
    return jnp.where(core == 0, mine, other), jnp.where(core == 0, other, mine)


def from_behind(value, steps):
    count = lax.axis_size("seq")
    first, last = max(0, -steps), min(count, count - steps)
    return lax.ppermute(value, "seq", [(s, s + steps) for s in range(first, last)])


def body(
    hidden, scene_lengths, norm_gain, w_in, conv_weight, conv_bias, dt_bias, a_log, d_skip,
    gate_gain, w_out, out_grad,
):
    tokens, model = hidden.shape
    heads = a_log.shape[0]
    inner = gate_gain.shape[0]
    channels = conv_bias.shape[0]
    state = (channels - inner) // 2
    chunks = tokens // Q
    repeat = LANES // heads
    columns = w_in.shape[1]

    scenes = scene_lengths.shape[0]
    order = jnp.arange(scenes)
    starts = jnp.sum(jnp.where(order[None, :] < order[:, None], scene_lengths[None, :], 0), axis=1)
    dev_start = lax.axis_index("seq") * tokens
    wide_pos = dev_start + jnp.arange(tokens + 8, dtype=jnp.int32)
    begin_all = jnp.max(jnp.where(starts[None, :] <= wide_pos[:, None], starts[None, :], 0), axis=1)
    begin, pos = begin_all[:tokens], wide_pos[:tokens]
    chunk_last = jnp.repeat(begin.reshape(chunks, Q)[:, -1], Q)
    chunk_start = pos // Q * Q
    inside = jnp.arange(tokens)
    notes = [
        begin,
        pos - 1 >= begin,
        pos - 2 >= begin,
        pos - 3 >= begin,
        (begin_all[1 : tokens + 1] <= pos) & (inside + 1 < tokens),
        (begin_all[2 : tokens + 2] <= pos) & (inside + 2 < tokens),
        (begin_all[3 : tokens + 3] <= pos) & (inside + 3 < tokens),
        begin == chunk_last,
        begin < chunk_start,
        begin < dev_start,
        begin != pos,
    ]
    meta = jnp.stack([n.astype(f32) for n in notes] + [jnp.zeros((tokens,), f32)] * (16 - len(notes)), axis=1)
    brow = begin.astype(f32).reshape(chunks, 1, Q)

    head_of = np.arange(inner) // (inner // heads)
    expand = np.arange(LANES)[:, None] % heads == head_of[None, :]
    expm, red = jnp.asarray(expand, bf16), jnp.asarray(expand.T, bf16)

    def four(v):
        return jnp.tile(v, repeat).reshape(1, LANES)

    gain_row = norm_gain.reshape(1, model)
    w_t = w_in.T
    w_dt = jnp.tile(w_t[inner + channels :], (repeat, 1)).T
    dsk = jnp.repeat(d_skip, inner // heads).reshape(1, inner)
    cb = conv_bias.reshape(1, channels)
    gate_row = gate_gain.reshape(1, inner)

    edge = hidden[tokens - 8 :].astype(f32)
    edge_low = (
        edge * lax.rsqrt(jnp.mean(edge * edge, axis=1, keepdims=True) + EPS) * norm_gain
    ).astype(bf16)
    edge_xbc = jnp.dot(
        edge_low, w_in[:, inner : inner + channels], preferred_element_type=f32
    ).astype(bf16)
    rim = from_behind(edge_xbc, 1).astype(f32)

    tb = SUB * Q
    whole = lambda shape: pl.BlockSpec(shape, lambda i: (0,) * len(shape), pipeline_mode=pl.Buffered(1))
    rowsb = lambda n, width: pl.BlockSpec((n, width), lambda i: (i, 0))
    sds = jax.ShapeDtypeStruct
    (nl, xbc, x, bc, dsil, step, sig, la, cum, decay, sloc, dev_state) = pl.pallas_call(
        functools.partial(project_kernel, heads, inner, state),
        grid=(tokens // tb,),
        in_specs=[
            rowsb(tb, model), whole((8, channels)), whole((1, model)),
            pl.BlockSpec((inner, model), lambda i: (1, 0), pipeline_mode=pl.Buffered(1)),
            pl.BlockSpec((2 * state, model), lambda i: (2 * inner // (2 * state), 0), pipeline_mode=pl.Buffered(1)),
            whole((model, LANES)), whole((4, channels)), whole((1, channels)), whole((1, LANES)),
            whole((1, LANES)), rowsb(tb, 16), whole((LANES, inner)),
        ],
        out_specs=[
            rowsb(tb, model), rowsb(tb, channels), rowsb(tb, inner), rowsb(tb, 2 * state),
            rowsb(tb, channels), rowsb(tb, LANES), rowsb(tb, LANES), rowsb(tb, LANES),
            rowsb(tb // Q * 8, LANES), rowsb(tb // Q * 8, inner),
            pl.BlockSpec((tb // Q, state, inner), lambda i: (i, 0, 0)),
            pl.BlockSpec((state, inner + LANES), lambda i: (0, 0)),
        ],
        out_shape=[
            sds((tokens, model), bf16), sds((tokens, channels), bf16), sds((tokens, inner), f32),
            sds((tokens, 2 * state), f32), sds((tokens, channels), f32), sds((tokens, LANES), f32),
            sds((tokens, LANES), f32), sds((tokens, LANES), f32), sds((chunks * 8, LANES), f32),
            sds((chunks * 8, inner), f32),
            sds((chunks, state, inner), f32), sds((state, inner + LANES), f32),
        ],
        scratch_shapes=[
            pltpu.VMEM((tb + 8, channels), f32), pltpu.VMEM((state, inner), f32), pltpu.VMEM((8, LANES), f32),
            pltpu.VMEM((3, tb, LANES), f32),
        ],
        compiler_params=params(),
        cost_estimate=cost(44),
    )(hidden, rim, gain_row, w_t, w_t, w_dt, conv_weight, cb, four(dt_bias), four(a_log), meta, expm)

    to_lanes = lambda d: jnp.repeat(d[..., :heads], inner // heads, axis=-1)
    got, notes = to_all(dev_state, inner)
    decays = to_lanes(notes)
    state_in = chain(got, decays, inner, False)

    z = jnp.dot(nl, w_in[:, :inner], preferred_element_type=f32)
    yss = pl.pallas_call(
        functools.partial(scan_kernel, heads, inner, state),
        grid=(chunks // SUB,),
        in_specs=[
            rowsb(tb, inner), rowsb(tb, 2 * state), rowsb(tb, LANES), rowsb(tb, LANES), rowsb(tb, 16),
            pl.BlockSpec((SUB, 1, Q), lambda i: (i, 0, 0)),
            pl.BlockSpec((SUB, state, inner), lambda i: (i, 0, 0)), whole((LANES, inner)),
        ],
        out_specs=rowsb(tb, inner),
        out_shape=sds((tokens, inner), f32),
        compiler_params=params(),
        cost_estimate=cost(41),
    )(x, bc, step, la, meta, brow, sloc, expm)

    gate_low, dy, gz, rowdot, state_in_grad, dgain, dskip = pl.pallas_call(
        functools.partial(gate_kernel, heads, inner, state),
        grid=(tokens // tb,),
        in_specs=[
            rowsb(tb, inner), rowsb(tb, inner), rowsb(tb, inner), rowsb(tb, model), whole((inner, model)),
            whole((state, inner)), rowsb(tb, 2 * state), rowsb(tb, LANES), rowsb(8 * SUB, LANES), rowsb(tb, 16),
            whole((1, inner)), whole((1, inner)), whole((LANES, inner)), whole((inner, LANES)),
        ],
        out_specs=[
            rowsb(tb, inner), rowsb(tb, inner), rowsb(tb, inner), rowsb(tb, LANES),
            pl.BlockSpec((state, inner + LANES), lambda i: (0, 0)), pl.BlockSpec((8, inner), lambda i: (0, 0)),
            pl.BlockSpec((8, inner), lambda i: (0, 0)),
        ],
        out_shape=[
            sds((tokens, inner), bf16), sds((tokens, inner), f32), sds((tokens, inner), bf16),
            sds((tokens, LANES), f32), sds((state, inner + LANES), f32), sds((8, inner), f32), sds((8, inner), f32),
        ],
        scratch_shapes=[
            pltpu.VMEM((tb, inner), f32), pltpu.VMEM((tb, inner), f32), pltpu.VMEM((3 * state, inner), bf16),
            pltpu.VMEM((tb, inner), f32), pltpu.VMEM((tb, inner), f32), pltpu.VMEM((8, model), f32),
        ],
        compiler_params=params(),
        cost_estimate=cost(50),
    )(yss, x, z, out_grad, w_out, state_in, bc, la, cum, meta, dsk, gate_row, expm, red)

    got, bounds = to_all(state_in_grad, inner)
    mixed_out = (hidden.astype(f32) + jnp.dot(gate_low, w_out, preferred_element_type=f32)).astype(bf16)
    normed_grad = jnp.einsum("te,de->td", gz, w_in[:, :inner], preferred_element_type=f32)
    state_out_grad = chain(got, decays, inner, True)
    state_out = dev_state[:, :inner] + to_lanes(dev_state[0:1, inner:]) * state_in

    core = lax.axis_index("seq") % 2
    contract = lambda left: lambda right: lax.dot_general(
        left, right, (((0,), (0,)), ((), ())), preferred_element_type=f32
    )
    halfc = inner // 2
    at = lambda v, c: lax.dynamic_slice_in_dim(v, c * halfc, halfc, 1)
    low_most = 1.02 * jnp.sqrt(jnp.float32(inner * tokens)) * jnp.max(jnp.abs(gate_gain))
    nl_most = 1.02 * jnp.sqrt(jnp.float32(model * tokens)) * jnp.max(jnp.abs(norm_gain))
    gz_bounds = jnp.sqrt(bounds[:, 0]) * nl_most
    og_bounds = jnp.sqrt(bounds[:, LANES - 1]) * low_most
    me = lax.axis_index("seq")
    flows = [
        Flow(chip_scatter(contract(out_grad), at(gate_low, core), at(gate_low, 1 - core), og_bounds[me], jnp.sum(og_bounds), (0, 1))),
        Flow(chip_scatter(contract(nl), at(gz, core), at(gz, 1 - core), gz_bounds[me], jnp.sum(gz_bounds), (1, 0))),
    ]

    final = chunks // SUB - 1
    width = 5 * LANES
    full = inner // width
    left_cols = inner - full * width
    conv_left = channels - full * width
    back = lambda n, cols: pl.BlockSpec((n, cols), lambda i: (final - i, 0))
    still = lambda shape: pl.BlockSpec(shape, lambda i: (0,) * len(shape))
    brow_spec = pl.BlockSpec((SUB, 1, Q), lambda i: (final - i, 0, 0))
    acc_specs = [back(tb, 4 * LANES), back(8 * SUB, LANES)]
    acc_shapes = [sds((tokens, 4 * LANES), f32), sds((chunks * 8, LANES), f32)]

    def back_group(g, dsk, acc, into):
        last_one = g == full
        w, wc = (left_cols, conv_left) if last_one else (width, width)
        b, bcv = (full * width // w, full * width // wc)if last_one else (g, g)
        chunk_cols = lambda n: pl.BlockSpec((n, w), lambda i: (final - i, b))
        conv_cols = lambda n: pl.BlockSpec((n, wc), lambda i: (final - i, bcv))
        fixed = lambda n, cols, block: pl.BlockSpec((n, cols), lambda i: (0, block), pipeline_mode=pl.Buffered(1))
        ins = [
            x, bc, step, la, decay, meta, brow, sloc, state_in, dy, dsil, xbc, state_out_grad,
            state_out, dsk, conv_weight, expm, red, *acc,
        ]
        specs = [
            chunk_cols(tb), back(tb, 2 * state), back(tb, LANES), back(tb, LANES), chunk_cols(8 * SUB),
            back(tb, 16), brow_spec, pl.BlockSpec((SUB, state, w), lambda i: (final - i, 0, b)),
            fixed(state, w, b), chunk_cols(tb), conv_cols(tb), conv_cols(tb), fixed(state, w, b),
            fixed(state, w, b), fixed(1, w, b), fixed(4, wc, bcv), fixed(LANES, w, b),
            pl.BlockSpec((w, LANES), lambda i: (b, 0), pipeline_mode=pl.Buffered(1)),
        ] + (acc_specs if acc else [])
        if last_one:
            ins += [sig, rowdot, four(a_log)]
            specs += [back(tb, LANES), back(tb, LANES), still((1, LANES))]
        aliases = {}
        if into is not None:
            aliases[len(ins)] = 0
            ins.append(into)
            specs.append(pl.BlockSpec(memory_space=pl.ANY))
        pg_spec = pl.BlockSpec((tb, width), lambda i: (final - i, g % 2))
        mid_specs, mid_shapes = (
            ([still((8, LANES))], [sds((8, LANES), f32)]) if last_one else (acc_specs, acc_shapes)
        )
        return pl.pallas_call(
            functools.partial(
                back_kernel, heads, inner // heads, state, g * width // (inner // heads), bool(acc),
                into is not None, last_one,
            ),
            grid=(chunks // SUB,),
            in_specs=specs,
            out_specs=[pg_spec] + mid_specs + [still((8, wc)), still((8, wc)), still((48, wc))],
            out_shape=[sds((tokens, 2 * width), bf16)]
            + mid_shapes
            + [sds((8, wc), f32), sds((8, wc), f32), sds((48, wc), f32)],
            scratch_shapes=[
                pltpu.VMEM((state, w), f32), pltpu.VMEM((tb + 8, wc), f32), pltpu.VMEM((8, LANES), f32),
                pltpu.VMEM((3, Q, LANES), f32),
            ],
            input_output_aliases=aliases,
            compiler_params=params(),
            cost_estimate=cost(20 if last_one else 38),
        )(*ins)

    ok_notes = jnp.stack(
        [(begin_all[tokens - 8 + j : tokens + j] <= wide_pos[tokens - 8 : tokens]).astype(f32) for j in range(4)], axis=1
    )

    def fix(part, rims, tails, sums, groups):
        at_last = pl.BlockSpec((16, 2 * width), lambda i: (tokens // 16 - 1, 0))
        ins, specs = [ok_notes, part], [whole((8, 4)), at_last]
        out_specs, shapes = [at_last], [sds(part.shape, bf16)]
        for rim_grad, tail, dcw, g in zip(rims, tails, sums, groups):
            w = tail.shape[1]
            b = g * width // w
            ins += [tail, rim_grad, conv_weight, xbc, dcw]
            specs += [
                whole((8, w)), whole((8, w)), pl.BlockSpec((4, w), lambda i, b=b: (0, b)),
                pl.BlockSpec((16, w), lambda i, b=b: (tokens // 16 - 1, b)), whole((48, w)),
            ]
            out_specs.append(pl.BlockSpec((8, w), lambda i: (0, 0)))
            shapes.append(sds((8, w), f32))
        out_specs.append(pl.BlockSpec((8, LANES), lambda i: (0, 0)))
        shapes.append(sds((8, LANES), f32))
        res = pl.pallas_call(
            functools.partial(edge_kernel, len(groups)), grid=(1,), in_specs=specs, out_specs=out_specs,
            out_shape=shapes, scratch_shapes=[pltpu.VMEM((16, width), f32)], input_output_aliases={1: 0},
            compiler_params=params(),
        )(*ins)
        return res[0], list(res[1:-1]), res[-1]

    reorder2 = lambda r: (r[1], r[0]) + tuple(r[2:])
    reorder = lambda r: (r[2],) + (r[0], r[1]) + tuple(r[3:])
    restore = lambda r: (r[1], r[2], r[0]) + tuple(r[3:])
    parts, rims, tails, sums = [], [], [], []
    acc, into = (), None
    for g in range(full):
        res = beside(flows, dsk, lambda m: reorder(back_group(g, m, acc, into)))
        part, a0, a1, first_g, tail_g, dcw_g = restore(res)
        acc = (a0, a1)
        rims.append(from_behind(first_g, -1))
        tails.append(tail_g)
        sums.append(dcw_g)
        into = part if g % 2 == 0 else None
        if g % 2 == 1:
            parts.append(part)
    part_a, dcws, near_a = fix(parts[0], rims[0:2], tails[0:2], sums[0:2], (0, 1))

    def bound_of(near):
        near = jnp.sqrt(near) * nl_most
        return near[0, 0], jnp.sum(trade(jnp.broadcast_to(near, (lax.axis_size("seq"), 8, LANES)))[:, 0, 0])

    own = lambda v, c: lax.dynamic_slice_in_dim(v, c * width, width, 1)
    flow_a = Flow(
        chip_scatter(contract(nl), own(part_a, core), own(part_a, 1 - core), *bound_of(near_a), (0, 1))
    )
    flows.append(flow_a)
    res = beside(flows, dsk, lambda m: reorder2(back_group(full, m, acc, into)))
    small, part, first_g, tail_g, dcw_g = res
    rims.append(from_behind(first_g, -1))
    part_b, dcw_b, near_b = fix(part, rims[2:], tails[2:] + [tail_g], sums[2:] + [dcw_g], (2, 3))
    bound_b = bound_of(jnp.maximum(near_b, jnp.max(small[2])))
    flow_b = Flow(
        chip_scatter(contract(nl), own(part_b, core), own(part_b, 1 - core), *bound_b, (1, 0))
    )
    dcw = jnp.concatenate(dcws + dcw_b, axis=1)

    cut = inner + 2 * width
    late = [flow_b, flow_a]
    part_a, part_b, away, kept = tie(part_a, part_b, *flow_b.value)
    flow_b.value = (away, kept)
    rest_of = lambda v: (
        normed_grad
        + jnp.dot(part_a, w_t[inner:cut], preferred_element_type=f32)
        + jnp.dot(v[:, : columns - cut], w_t[cut:], preferred_element_type=f32),
    )
    (normed_all,) = beside(late, part_b, rest_of)
    normed_all, dcw, small, out_done, z_done = tie(
        normed_all, dcw, small, flows[0].finish(), flows[1].finish()
    )
    conv_weight_part = dcw[0:4]

    def into_hidden(normed_grad):
        hv = hidden.astype(f32)
        s = lax.rsqrt(jnp.mean(hv * hv, axis=1, keepdims=True) + EPS)
        gained = normed_grad * norm_gain
        inner_mean = jnp.mean(gained * hv, axis=1, keepdims=True)
        hidden_grad = out_grad.astype(f32) + s * gained - hv * (s * s * s * inner_mean)
        return jnp.sum(normed_grad * hv * s, axis=0), hidden_grad

    norm_gain_part, hidden_grad = beside(late, normed_all, into_hidden)
    out_rows = jnp.concatenate(both_cores(out_done), axis=1)
    w_out_grad = out_rows.T
    z_rows = both_cores(z_done)
    a_rows = both_cores(flow_a.finish())
    b_rows = both_cores(flow_b.finish())
    w_in_grad = jnp.concatenate(list(z_rows) + list(a_rows) + list(b_rows), axis=1)[:, :columns]

    dskip_part = jnp.sum(dskip[0].reshape(heads, inner // heads), axis=1)
    early = (conv_weight_part.reshape(-1), dcw[4], small[1, :heads], small[0, :heads], dskip_part, dgain[0])
    total = sum_all(jnp.concatenate(early))
    summed, start = [], 0
    for part in early:
        summed.append(total[start : start + part.shape[0]])
        start += part.shape[0]
    norm_gain_grad = sum_all_once(norm_gain_part)
    return (
        mixed_out, hidden_grad, norm_gain_grad, w_in_grad, summed[0].reshape(conv_weight.shape), summed[1],
        summed[2], summed[3], summed[4], summed[5], w_out_grad,
    )


def solution(mesh):
    rep = P()
    return jax.shard_map(
        body,
        mesh=mesh,
        in_specs=(P("seq", None),) + (rep,) * 10 + (P("seq", None),),
        out_specs=(P("seq", None), P("seq", None), rep, P("seq", None), rep, rep, rep, rep, rep, rep, P(None, "seq")),
        check_vma=False,
    )
```
